256 devices in a mesh: dp: 32 (over x, z), head: 8 (over y, core).
Axes of the slice: x: 4, y: 4, z: 8, core: 2. Of those that a mesh axis runs over, the one named last changes fastest.
Arguments:
- key_grads: bfloat16 [2, 16384, 2048], P(None, 'dp', 'head'), may hold values from -6 to 6
- value_grads: bfloat16 [2, 16384, 2048], P(None, 'dp', 'head'), may hold values from -6 to 6
- key_weight: bfloat16 [2, 3584, 2048], P(None, 'dp', 'head'), may hold values from -0.125 to 0.125
- value_weight: bfloat16 [2, 3584, 2048], P(None, 'dp', 'head'), may hold values from -0.125 to 0.125
- block_source: int32 [1024], replicated, may hold values from 0 to 1023, as said below
- hidden_mid: bfloat16 [16384, 3584], P('dp', 'head')
- mlp_out: bfloat16 [16384, 3584], P('dp', 'head')
- post_gain: bfloat16 [3584], P('head'), may hold values from 0.5 to 2
- final_gain: bfloat16 [3584], P('head'), may hold values from 0.5 to 2
- gate_pre: bfloat16 [16384, 7168], P('dp', 'head'), may hold values from -6 to 6
- up_pre: bfloat16 [16384, 7168], P('dp', 'head'), may hold values from -6 to 6
- down_weight: bfloat16 [7168, 3584], P('head', 'dp'), may hold values from -0.09375 to 0.09375
Outputs:
- resid_grad: bfloat16 [16384, 3584], P('dp', 'head')
- gate_grad: bfloat16 [16384, 7168], P('dp', 'head')
- up_grad: bfloat16 [16384, 7168], P('dp', 'head')
The draws below stay inside these ranges and needn't reach their ends.
Inputs may be any that keep to these rules, and one draw needn't show every extreme that they name: block_source is a permutation of the 1024 row blocks. The decoder blocks of one device are blocks 32 * a to 32 * a + 31, and the encoder blocks of device b are blocks 32 * b to 32 * b + 31; at most 2 decoder blocks of one device fill encoder blocks of one device, and exactly 2 do for some pairs of devices in every draw.
All inputs are finite; a program needn't handle non-finite values.
Results may differ from the reference program's by a relative error of at most 0.02.
Values may be sent and summed in bfloat16 or wider, within the bound.
No kernel may reach another device: no remote copies, remote signals or barrier semaphores. Data moves between devices by JAX's collectives and lax.ppermute only.
A program may use at most 64 MiB of HBM per device.

```python
import math
import jax
import jax.numpy as jnp
from jax import lax

D = 3584
KVH = 8
HD = 256
FFW = 7168
XL = 2
CAP = 2
TOKENS = 16384
BLK = 16
NBLK = 1024
N_DP = 32
N_HEAD = 8


def field_scales(scale_key):
    row_key, col_key = jax.random.split(scale_key)
    row_scale = jnp.exp(jax.random.uniform(row_key, (TOKENS, 1), jnp.float32) * math.log(10.0))
    col_ramp = jnp.arange(D, dtype=jnp.float32)[None, :] / D * math.log(3.0)
    col_scale = jnp.exp(jax.random.uniform(col_key, (1, D), jnp.float32) * math.log(10.0) + col_ramp)
    return row_scale * col_scale


def draw_hidden_mid(key, part):
    key = jax.random.fold_in(key, 11)
    scale_key, value_key = jax.random.split(key, 2)
    scales = field_scales(scale_key) * 0.25
    values = jax.random.normal(value_key, (TOKENS, D), jnp.float32)
    return (values * scales).astype(jnp.bfloat16)


def draw_mlp_out(key, part):
    key = jax.random.fold_in(key, 23)
    scale_key, value_key = jax.random.split(key, 2)
    scales = field_scales(scale_key) * 0.25
    values = jax.random.normal(value_key, (TOKENS, D), jnp.float32)
    return (values * scales).astype(jnp.bfloat16)


def draw_block_source(key, part):
    key = jax.random.fold_in(key, 5)
    device_key, shift_key, slot_key, order_key = jax.random.split(key, 4)
    device_perm = jax.random.permutation(device_key, N_DP)
    device_shift = jax.random.permutation(shift_key, N_DP)
    slot_keys = jax.random.split(slot_key, N_DP)
    slot_perm = jax.vmap(lambda one_key: jax.random.permutation(one_key, N_DP))(slot_keys)
    group_of = slot_perm // CAP
    dest_device = device_perm[(device_shift[:, None] + group_of) % N_DP]
    flat_dest = dest_device.reshape(-1).astype(jnp.int32)
    priority = jax.random.permutation(order_key, NBLK)
    earlier = (flat_dest[:, None] == flat_dest[None, :]) & (priority[None, :] < priority[:, None])
    dest_slot = jnp.sum(earlier.astype(jnp.int32), axis=1).astype(jnp.int32)
    dest_block = flat_dest * N_DP + dest_slot
    return jnp.argsort(dest_block).astype(jnp.int32)


def block_levels(rng, extent, shards, smallest, top_value):
    def one(axis_at, shards_of):
        heights = jax.random.uniform(jax.random.fold_in(jax.random.fold_in(rng, 6), axis_at), (shards_of,), jnp.float32, smallest / len(shards), top_value / len(shards))
        return jnp.repeat(jnp.exp(heights), extent[axis_at] // shards_of).reshape((-1,) + (1,) * (len(extent) - axis_at - 1))

    factor_of = one(*shards[0])
    for cut in shards[1:]:
        factor_of = factor_of * one(*cut)
    return factor_of


def gaussian(own_key, shape, width, most, cuts=(), kind=jnp.bfloat16):
    level = block_levels(own_key, shape, cuts, -0.22, 0.18) if cuts else 1.0
    array = jax.random.normal(own_key, shape, jnp.float32) * width * level
    return jnp.minimum(jnp.maximum(array, -most), most).astype(kind)


def setup_inputs(seed: int = 0) -> dict:
    streams_of = jax.random.split(jax.random.key(seed), 13)
    key_grads = gaussian(streams_of[0], (XL, TOKENS, KVH * HD), 1.0, 6.0, ((1, 32), (2, 8)))
    value_grads = gaussian(streams_of[1], (XL, TOKENS, KVH * HD), 1.0, 6.0, ((1, 32), (2, 8)))
    key_weight = gaussian(streams_of[2], (XL, D, KVH * HD), (KVH * HD) ** -0.5, 0.125, ((1, 32), (2, 8)))
    value_weight = gaussian(streams_of[3], (XL, D, KVH * HD), (KVH * HD) ** -0.5, 0.125, ((1, 32), (2, 8)))
    block_source = draw_block_source(jax.random.fold_in(streams_of[12], 71), 0)
    hidden_mid = draw_hidden_mid(jax.random.fold_in(streams_of[12], 71), 0)
    mlp_out = draw_mlp_out(jax.random.fold_in(streams_of[12], 71), 0)
    post_gain = jnp.clip(jnp.exp(math.log(2.0) - 1.3862944 * jax.random.uniform(streams_of[7], (D,), jnp.float32) ** block_levels(streams_of[7], (D,), ((0, 8),), -0.2, 0.2)), 0.5, 2.0).astype(jnp.bfloat16)
    final_gain = jnp.clip(jnp.exp(math.log(2.0) - 1.3862944 * jax.random.uniform(streams_of[8], (D,), jnp.float32) ** block_levels(streams_of[8], (D,), ((0, 8),), -0.2, 0.2)), 0.5, 2.0).astype(jnp.bfloat16)
    gate_pre = gaussian(streams_of[9], (TOKENS, FFW), 1.5, 6.0, ((0, 32), (1, 8)))
    up_pre = gaussian(streams_of[10], (TOKENS, FFW), 1.5, 6.0, ((0, 32), (1, 8)))
    down_weight = gaussian(streams_of[11], (FFW, D), D ** -0.5, 0.09375, ((0, 8), (1, 32)))
    return {"key_grads": key_grads, "value_grads": value_grads, "key_weight": key_weight, "value_weight": value_weight, "block_source": block_source, "hidden_mid": hidden_mid, "mlp_out": mlp_out, "post_gain": post_gain, "final_gain": final_gain, "gate_pre": gate_pre, "up_pre": up_pre, "down_weight": down_weight}


epsilon = 1e-06

def gelu_parts(gate_value):
    activated, pullback = jax.vjp(lambda pre_act: jax.nn.gelu(pre_act, approximate=True), gate_value)
    return (activated, pullback(jnp.ones_like(gate_value))[0])

def reference(key_grads, value_grads, key_weight, value_weight, block_source, hidden_mid, mlp_out, post_gain, final_gain, gate_pre, up_pre, down_weight):
    group_cols = KVH * HD // N_HEAD
    memory_sum = jnp.zeros((TOKENS, D), jnp.float32)
    for group in range(N_HEAD):
        low = group * group_cols
        high = low + group_cols
        group_sum = jnp.zeros((TOKENS, D), jnp.float32)
        for layer in range(XL):
            group_sum = group_sum + jnp.dot(key_grads[layer][:, low:high], key_weight[layer][:, low:high].T, preferred_element_type=jnp.float32)
            group_sum = group_sum + jnp.dot(value_grads[layer][:, low:high], value_weight[layer][:, low:high].T, preferred_element_type=jnp.float32)
        memory_sum = memory_sum + group_sum.astype(jnp.bfloat16).astype(jnp.float32)
    dec_memory = memory_sum.astype(jnp.bfloat16)
    memory_grad = dec_memory.reshape(NBLK, BLK, D)[block_source.astype(jnp.int32)].reshape(TOKENS, D)
    mid_value = hidden_mid.astype(jnp.float32)
    out_value = mlp_out.astype(jnp.float32)
    gain_post = post_gain.astype(jnp.float32)
    gain_final = final_gain.astype(jnp.float32)
    out_scale = lax.rsqrt(lax.optimization_barrier(jnp.mean(out_value * out_value, axis=1, keepdims=True)) + epsilon)
    resid = mid_value + out_value * out_scale * gain_post
    resid_scale = lax.rsqrt(lax.optimization_barrier(jnp.mean(resid * resid, axis=1, keepdims=True)) + epsilon)
    norm_grad = memory_grad.astype(jnp.float32) * gain_final
    final_mean = resid_scale * lax.optimization_barrier(jnp.mean(norm_grad * resid, axis=1, keepdims=True))
    resid_total = resid_scale * (norm_grad - resid * resid_scale * final_mean)
    post_input = resid_total * gain_post
    post_mean = out_scale * lax.optimization_barrier(jnp.mean(post_input * out_value, axis=1, keepdims=True))
    post_grad = (out_scale * (post_input - out_value * out_scale * post_mean)).astype(jnp.bfloat16)
    hidden_grad = jnp.dot(post_grad, down_weight.T, preferred_element_type=jnp.float32)
    activated, slope = gelu_parts(gate_pre.astype(jnp.float32))
    gate_grad = (hidden_grad * up_pre.astype(jnp.float32) * slope).astype(jnp.bfloat16)
    up_grad = (hidden_grad * activated).astype(jnp.bfloat16)
    return (resid_total.astype(jnp.bfloat16), gate_grad, up_grad)
```

```python
import jax
import jax.numpy as jnp
from jax import lax
from jax.experimental import pallas as pl
from jax.experimental.pallas import tpu as pltpu
from jax.sharding import PartitionSpec as P

EPS = 1e-06
NX, NZ, NY, NC = 4, 8, 4, 2
AXES = ("dp", "head")
BF = jnp.bfloat16
F32 = jnp.float32
VMEM_LIMIT = 56 * 1024 * 1024


def move(value, dx=0, dz=0, dy=0, dc=0):
    pairs = []
    for x in range(NX):
        for z in range(NZ):
            for y in range(NY):
                for c in range(NC):
                    src = (x * NZ + z) * 8 + y * NC + c
                    dst = (
                        ((x + dx) % NX * NZ + (z + dz) % NZ) * 8
                        + (y + dy) % NY * NC
                        + (c + dc) % NC
                    )
                    pairs.append((src, dst))
    return lax.ppermute(value, AXES, pairs)


def spread_columns(shard):
    pairs = []
    for x in range(NX):
        for z in range(NZ):
            for head in range(8):
                c, t = z // 4, z % 4
                pairs.append(((x * NZ + z) * 8 + head, (t * NZ + 4 * c + x) * 8 + head))
    return lax.ppermute(shard, AXES, pairs)


def call(kernel, out_shape, n_scalar, n_array, flops, scratch=(), name=None):
    return pl.pallas_call(
        kernel,
        out_shape=out_shape,
        in_specs=[pl.BlockSpec(memory_space=pltpu.SMEM)] * n_scalar
        + [pl.BlockSpec(memory_space=pltpu.VMEM)] * n_array,
        out_specs=jax.tree.map(lambda _: pl.BlockSpec(memory_space=pltpu.VMEM), out_shape),
        scratch_shapes=scratch,
        compiler_params=pltpu.CompilerParams(vmem_limit_bytes=VMEM_LIMIT),
        cost_estimate=pl.CostEstimate(flops=flops, bytes_accessed=6_000_000, transcendentals=0),
        name=name,
    )


def dot_nt(a, b):
    return lax.dot_general(a, b, (((1,), (1,)), ((), ())), preferred_element_type=F32)


def dot_tn(a, b):
    return lax.dot_general(a, b, (((0,), (0,)), ((), ())), preferred_element_type=F32)


def part_kernel(slot, w0, f1, f2, f3, g1, g2, g3, oa, ob, r0, r1, r2, r3a, r3b, out, wall):
    for k, ref in enumerate((w0, f1, f2, f3, g1, g2, g3)):
        wall[k * 112 : (k + 1) * 112, :] = ref[...]
    wall[784:848, :] = oa[...]
    wall[848:896, :] = ob[...]
    at = 0
    for ref in (r0, r1, r2, r3a, r3b):
        size = ref.shape[0]
        prod = dot_nt(wall[...], ref[...]).astype(BF)
        for k in range(8):
            out[slot[k], :, at : at + size] = prod[k * 112 : (k + 1) * 112, :]
        at += size


def send_kernel(xs, parts, lane_pos, out, moved):
    for r in range(4):
        total = parts[0, :, r * 512 : (r + 1) * 512].astype(F32)
        for g in range(1, 8):
            total = total + parts[g, :, r * 512 : (r + 1) * 512].astype(F32)
        ids = lax.broadcasted_iota(jnp.int32, (1024, 512), 0)
        pick = jnp.where(ids == lane_pos[r : r + 1, :], 1.0, 0.0).astype(BF)
        moved[xs[r]] = dot_nt(total.astype(BF), pick).astype(BF)
    group = lax.broadcasted_iota(jnp.int32, (112, 128), 1) // 32
    for q in range(8):
        tiles = [moved[x, :, q * 128 : (q + 1) * 128] for x in range(4)]
        for j in range(4):
            here = tiles[(0 - j) % 4]
            for g in range(1, 4):
                here = jnp.where(group == g, tiles[(g - j) % 4], here)
            out[4 * q + j] = here


def recv_kernel(arrived, row_pos, resid, gout, gain_final, grad, dots):
    ids = lax.broadcasted_iota(jnp.int32, (1024, 512), 0)
    pick = jnp.where(ids == row_pos[...], 1.0, 0.0).astype(BF)
    first = jnp.zeros((1, 512), F32)
    second = jnp.zeros((1, 512), F32)
    for x in range(4):
        side = jnp.concatenate([arrived[x * 8 + z] for z in range(8)], axis=1)
        rows = pl.ds(x * 112, 112)
        piece = jnp.dot(side, pick, preferred_element_type=F32)
        piece = piece * gain_final[rows, :]
        grad[rows, :] = piece
        first = first + jnp.sum(piece * resid[rows, :], axis=0, keepdims=True)
        second = second + jnp.sum(piece * gout[rows, :], axis=0, keepdims=True)
    dots[0:1, :] = first
    dots[1:2, :] = second


def norm_kernel(norm_grad, resid, out_value, gain_post, stats, dots, resid_grad, post_grad):
    width = 3584.0
    out_scale = stats[0:1, :]
    resid_scale = stats[1:2, :]
    cross = stats[2:3, :]
    both = dots[0]
    for k in range(1, 8):
        both = both + dots[k]
    final_mean = resid_scale * both[0:1, :] / width
    post_dot = resid_scale * (both[1:2, :] - resid_scale * final_mean * cross)
    post_mean = out_scale * post_dot / width
    total = resid_scale * (norm_grad[...] - resid[...] * (resid_scale * final_mean))
    post = out_scale * (total * gain_post[...] - out_value[...] * (out_scale * post_mean))
    post_grad[...] = post.astype(BF)
    resid_grad[...] = total.T.astype(BF)


def final_kernel(heads, p0, p1, p2, p3, p4, p5, p6, p7, weight, slope, active, gate, up):
    total = jnp.zeros((512, 896), F32)
    for k, ref in enumerate((p0, p1, p2, p3, p4, p5, p6, p7)):
        rows = pl.ds(pl.multiple_of(heads[k] * 448, 64), 448)
        total = total + dot_tn(ref[...], weight[rows, :])
    gate[...] = (total * slope[...]).astype(BF)
    up[...] = (total * active[...]).astype(BF)


def gelu_parts(gate_value):
    activated, pullback = jax.vjp(
        lambda pre_act: jax.nn.gelu(pre_act, approximate=True), gate_value
    )
    return (activated, pullback(jnp.ones_like(gate_value))[0])


def swap_rows(value):
    return lax.all_to_all(
        jnp.broadcast_to(value[None], (8,) + value.shape), "head", 0, 0, tiled=True
    )


def per_device(
    key_grads,
    value_grads,
    key_weight,
    value_weight,
    block_source,
    hidden_mid,
    mlp_out,
    post_gain,
    final_gain,
    gate_pre,
    up_pre,
    down_weight,
):
    dev = lax.axis_index("dp")
    head = lax.axis_index("head")
    x, z = dev // NZ, dev % NZ
    y, c = head // NC, head % NC

    weight = jnp.concatenate([key_weight[0], key_weight[1], value_weight[0], value_weight[1]], 1)
    rows = jnp.concatenate([key_grads[0], key_grads[1], value_grads[0], value_grads[1]], 1)
    r1 = move(rows, dx=1)
    r2 = move(rows, dx=-1)
    w0 = spread_columns(weight)
    f1, g1 = move(w0, dz=1), move(w0, dz=-1)
    f2, g2 = move(f1, dz=1), move(g1, dz=-1)
    f3, g3 = move(f2, dz=1), move(g2, dz=-1)
    oa, ob = move(f3[:64], dz=1), move(g3[64:], dz=-1)
    r3a = move(r1[:256], dx=1)
    r3b = move(r2[256:], dx=-1)

    block_ids = jnp.arange(1024, dtype=jnp.int32)
    is_source = block_source[:, None] == block_ids[None, :]
    dest_block = jnp.sum(jnp.where(is_source, block_ids[:, None], 0), axis=0)
    dest_device = (dest_block // 32).reshape(32, 32)
    same_dest = dest_device[:, :, None] == dest_device[:, None, :]
    slot_ids = jnp.arange(32, dtype=jnp.int32)
    before = slot_ids[None, :] < slot_ids[:, None]
    rank = jnp.sum((same_dest & before[None]).astype(jnp.int32), axis=2)
    own_x = jnp.stack([x, (x + 3) % 4, (x + 1) % 4, (x + 2) % 4]).astype(jnp.int32)
    dest_own = dest_device[own_x * NZ + z]
    rank_own = rank[own_x * NZ + z]
    lanes = (
        (dest_own // 4) * 128 + ((dest_own % 4 + own_x[:, None]) % 4) * 32 + rank_own * 16
    )
    lane_pos = (lanes[:, :, None] + jnp.arange(16, dtype=jnp.int32)).reshape(4, 512)
    source = lax.dynamic_slice_in_dim(block_source, dev * 32, 32)
    source_dev = source // 32
    source_rank = jnp.sum(
        jnp.where(block_ids[None, :] == source[:, None], rank.reshape(-1)[None, :], 0), axis=1
    )
    spot = (
        (source_dev % NZ) * 128 + ((dev % 4 + source_dev // NZ) % 4) * 32 + source_rank * 16
    )
    row_pos = (spot[:, None] + jnp.arange(16, dtype=jnp.int32)).reshape(1, 512)

    gain_post = post_gain.astype(F32)[:, None]
    gain_final = final_gain.astype(F32)[:, None]
    out_value = mlp_out.T.astype(F32)
    mid_value = hidden_mid.T.astype(F32)
    sum_out = jnp.sum(swap_rows(jnp.sum(out_value * out_value, axis=0)[None]), axis=0)
    out_scale = lax.rsqrt(sum_out / 3584 + EPS)
    gout = out_value * gain_post
    resid = mid_value + gout * out_scale
    pair = jnp.stack([jnp.sum(resid * resid, axis=0), jnp.sum(resid * gout, axis=0)])
    pair = jnp.sum(swap_rows(pair), axis=0)
    resid_scale = lax.rsqrt(pair[0:1] / 3584 + EPS)
    stats = jnp.concatenate([out_scale, resid_scale, pair[1:2]], axis=0)
    active, slope = gelu_parts(gate_pre.astype(F32))
    slope = slope * up_pre.astype(F32)
    down = lax.all_gather(down_weight.T, "dp", axis=0, tiled=True)

    pos = (z - jnp.array([0, 1, 2, 3, -1, -2, -3, 4], jnp.int32)) % NZ
    slot = (2 * (pos % 4) + pos // 4).astype(jnp.int32)
    parts = call(
        part_kernel,
        jax.ShapeDtypeStruct((8, 112, 2048), BF),
        1,
        14,
        2 * 2048 * 896 * 1024,
        [pltpu.VMEM((896, 1024), BF)],
        name="part",
    )(slot, w0, f1, f2, f3, g1, g2, g3, oa, ob, rows, r1, r2, r3a, r3b)
    parts = lax.all_to_all(parts, "head", 0, 0, tiled=True)
    outgoing = call(
        send_kernel,
        jax.ShapeDtypeStruct((32, 112, 128), BF),
        1,
        2,
        2 * 112 * 2048 * 1024,
        [pltpu.VMEM((4, 112, 1024), BF)],
        name="send",
    )(own_x, parts, lane_pos)
    arrived = lax.all_to_all(outgoing, "dp", 0, 0, tiled=True)
    norm_grad, dots = call(
        recv_kernel,
        (jax.ShapeDtypeStruct((448, 512), F32), jax.ShapeDtypeStruct((2, 512), F32)),
        0,
        5,
        2 * 448 * 512 * 1024,
        name="recv",
    )(arrived, row_pos, resid, gout, gain_final)
    dots = swap_rows(dots)
    resid_grad, post = call(
        norm_kernel,
        (jax.ShapeDtypeStruct((512, 448), BF), jax.ShapeDtypeStruct((448, 512), BF)),
        0,
        6,
        448 * 512 * 20,
        name="norm",
    )(norm_grad, resid, out_value, gain_post, stats, dots)
    s0 = move(post, dc=1)
    p1, p2, p3 = move(post, dy=1), move(post, dy=-1), move(post, dy=2)
    s1, s2, s3 = move(p1, dc=1), move(p2, dc=1), move(p3, dc=1)
    from_y = jnp.stack([y, y, y + 3, y + 3, y + 1, y + 1, y + 2, y + 2]) % 4
    from_c = (c + jnp.array([0, 1] * 4, jnp.int32)) % 2
    heads = (from_y * 2 + from_c).astype(jnp.int32)
    gate_grad, up_grad = call(
        final_kernel,
        (jax.ShapeDtypeStruct((512, 896), BF), jax.ShapeDtypeStruct((512, 896), BF)),
        1,
        11,
        2 * 512 * 896 * 3584,
        name="final",
    )(heads, post, s0, p1, s1, p2, s2, p3, s3, down, slope, active)
    return (resid_grad, gate_grad, up_grad)


def solution(mesh):
    return jax.shard_map(
        per_device,
        mesh=mesh,
        in_specs=(
            P(None, "dp", "head"),
            P(None, "dp", "head"),
            P(None, "dp", "head"),
            P(None, "dp", "head"),
            P(),
            P("dp", "head"),
            P("dp", "head"),
            P("head"),
            P("head"),
            P("dp", "head"),
            P("dp", "head"),
            P("head", "dp"),
        ),
        out_specs=(P("dp", "head"), P("dp", "head"), P("dp", "head")),
        check_vma=False,
    )
```

```python
import jax
import jax.numpy as jnp
from jax import lax
from jax.experimental import pallas as pl
from jax.experimental.pallas import tpu as pltpu
from jax.sharding import PartitionSpec as P

EPS = 1e-06
NX, NZ, NY, NC = 4, 8, 4, 2
AXES = ("dp", "head")
BF = jnp.bfloat16
F32 = jnp.float32
MIB = 56
W_FIRST = 0
R3 = 1
TIE = 1


def move(value, dx=0, dz=0, dy=0, dc=0):
    pairs = []
    for x in range(NX):
        for z in range(NZ):
            for y in range(NY):
                for c in range(NC):
                    src = (x * NZ + z) * 8 + y * NC + c
                    dst = (
                        ((x + dx) % NX * NZ + (z + dz) % NZ) * 8
                        + (y + dy) % NY * NC
                        + (c + dc) % NC
                    )
                    pairs.append((src, dst))
    return lax.ppermute(value, AXES, pairs)


def spread_columns(shard):
    pairs = []
    for x in range(NX):
        for z in range(NZ):
            for y in range(NY):
                for c in range(NC):
                    d, t = z // 4, z % 4
                    src = (x * NZ + z) * 8 + y * NC + c
                    pairs.append((src, (t * NZ + 4 * c + x) * 8 + y * NC + d))
    return lax.ppermute(shard, AXES, pairs)


def call(kernel, out_shape, n_scalar, n_array, flops, scratch=(), name=None, space=pltpu.VMEM):
    return pl.pallas_call(
        kernel,
        out_shape=out_shape,
        in_specs=[pl.BlockSpec(memory_space=pltpu.SMEM)] * n_scalar
        + [pl.BlockSpec(memory_space=space)] * n_array,
        out_specs=jax.tree.map(lambda _: pl.BlockSpec(memory_space=pltpu.VMEM), out_shape),
        scratch_shapes=scratch,
        compiler_params=pltpu.CompilerParams(vmem_limit_bytes=MIB * 1024 * 1024),
        cost_estimate=pl.CostEstimate(flops=flops, bytes_accessed=6_000_000, transcendentals=0),
        name=name,
    )


def dot_nt(a, b):
    return lax.dot_general(a, b, (((1,), (1,)), ((), ())), preferred_element_type=F32)


def dot_tn(a, b):
    return lax.dot_general(a, b, (((0,), (0,)), ((), ())), preferred_element_type=F32)


def part_kernel(where, core, *refs):
    pieces, out, wall, rows, sems = refs[:8], refs[-4], refs[-3], refs[-2], refs[-1]
    count = (len(refs) - 12) // 2
    copies = []
    for k, ref in enumerate(pieces):
        at = pl.multiple_of(where[k] % 4 * 112, 16)
        spot = wall.at[where[k] // 4, pl.ds(at, 112)]
        copies.append(pltpu.make_async_copy(ref, spot, sems.at[k]))
    at = 0
    for k in range(count):
        size = refs[8 + k].shape[0]
        for side in range(2):
            spot = rows.at[side, pl.ds(at, size)]
            ref, sem = refs[8 + side * count + k], sems.at[8 + 2 * k + side]
            copies.append(pltpu.make_async_copy(ref, spot, sem))
        at += size
    for copy in copies:
        copy.start()
    for copy in copies[:8]:
        copy.wait()
    own, other = wall[core[0]], wall[1 - core[0]]
    at = 0
    for k in range(count):
        size = refs[8 + k].shape[0]
        copies[8 + 2 * k].wait()
        copies[9 + 2 * k].wait()
        prod = dot_nt(own, rows[0, at : at + size, :])
        prod = (prod + dot_nt(other, rows[1, at : at + size, :])).astype(BF)
        for y in range(4):
            out[y, :, at : at + size] = prod[y * 112 : (y + 1) * 112, :]
        at += size


def send_kernel(xs, first, last, lane_pos, out, moved):
    for r in range(4):
        parts, at = (first, r * 512) if r < 3 else (last, 0)
        total = parts[0, :, at : at + 512].astype(F32)
        for g in range(1, 4):
            total = total + parts[g, :, at : at + 512].astype(F32)
        ids = lax.broadcasted_iota(jnp.int32, (1024, 512), 0)
        pick = jnp.where(ids == lane_pos[r : r + 1, :], 1.0, 0.0).astype(BF)
        moved[xs[r]] = dot_nt(total.astype(BF), pick).astype(BF)
    group = lax.broadcasted_iota(jnp.int32, (112, 128), 1) // 32
    for q in range(8):
        tiles = [moved[x, :, q * 128 : (q + 1) * 128] for x in range(4)]
        for j in range(4):
            here = tiles[(0 - j) % 4]
            for g in range(1, 4):
                here = jnp.where(group == g, tiles[(g - j) % 4], here)
            out[4 * q + j] = here


def recv_kernel(arrived, row_pos, resid, gout, gain_final, pair, grad, dots):
    ids = lax.broadcasted_iota(jnp.int32, (1024, 512), 0)
    pick = jnp.where(ids == row_pos[...], 1.0, 0.0).astype(BF)
    first = jnp.zeros((1, 512), F32)
    second = jnp.zeros((1, 512), F32)
    for x in range(4):
        side = jnp.concatenate([arrived[x * 8 + z] for z in range(8)], axis=1)
        rows = pl.ds(x * 112, 112)
        piece = jnp.dot(side, pick, preferred_element_type=F32)
        piece = piece * gain_final[rows, :]
        grad[rows, :] = piece
        first = first + jnp.sum(piece * resid[rows, :], axis=0, keepdims=True)
        second = second + jnp.sum(piece * gout[rows, :], axis=0, keepdims=True)
    for k in range(8):
        dots[k, 0:1, :] = first
        dots[k, 1:2, :] = second
        dots[k, 2:4, :] = pair[...]


def norm_kernel(norm_grad, resid, out_value, gain_post, out_scale, dots, resid_grad, post_grad):
    width = 3584.0
    sums = dots[0]
    for k in range(1, 8):
        sums = sums + dots[k]
    out_scale = out_scale[...]
    resid_scale = lax.rsqrt(sums[2:3, :] / width + EPS)
    final_mean = resid_scale * sums[0:1, :] / width
    post_dot = resid_scale * (sums[1:2, :] - resid_scale * final_mean * sums[3:4, :])
    post_mean = out_scale * post_dot / width
    total = resid_scale * (norm_grad[...] - resid[...] * (resid_scale * final_mean))
    post = out_scale * (total * gain_post[...] - out_value[...] * (out_scale * post_mean))
    post_grad[...] = post.astype(BF)
    resid_grad[...] = total.T.astype(BF)


def final_kernel(heads, *refs):
    posts, (weight, slope, active, gate, up) = refs[:8], refs[8:13]
    post_buf, weight_buf, scale_buf, sems = refs[13:]
    copies = []
    for k in range(8):
        at = pl.multiple_of(heads[k] * 448, 64)
        copies.append(pltpu.make_async_copy(posts[k], post_buf.at[k], sems.at[2 * k]))
        rows = weight.at[pl.ds(at, 448)]
        copies.append(pltpu.make_async_copy(rows, weight_buf.at[k], sems.at[2 * k + 1]))
    copies.append(pltpu.make_async_copy(slope, scale_buf.at[0], sems.at[16]))
    copies.append(pltpu.make_async_copy(active, scale_buf.at[1], sems.at[17]))
    for copy in copies:
        copy.start()
    value = jnp.zeros((512, 896), F32)
    for k in range(8):
        copies[2 * k].wait()
        copies[2 * k + 1].wait()
        value = value + dot_tn(post_buf[k], weight_buf[k])
    copies[16].wait()
    copies[17].wait()
    gate[...] = (value * scale_buf[0]).astype(BF)
    up[...] = (value * scale_buf[1]).astype(BF)


def gelu_parts(gate_value):
    activated, pullback = jax.vjp(
        lambda pre_act: jax.nn.gelu(pre_act, approximate=True), gate_value
    )
    return (activated, pullback(jnp.ones_like(gate_value))[0])


def swap_rows(value):
    return lax.all_to_all(
        jnp.broadcast_to(value[None], (8,) + value.shape), "head", 0, 0, tiled=True
    )


def per_device(
    key_grads,
    value_grads,
    key_weight,
    value_weight,
    block_source,
    hidden_mid,
    mlp_out,
    post_gain,
    final_gain,
    gate_pre,
    up_pre,
    down_weight,
):
    dev = lax.axis_index("dp")
    head = lax.axis_index("head")
    x, z = dev // NZ, dev % NZ
    y, c = head // NC, head % NC

    weight = jnp.concatenate([key_weight[0], key_weight[1], value_weight[0], value_weight[1]], 1)
    rows = jnp.concatenate([key_grads[0], key_grads[1], value_grads[0], value_grads[1]], 1)
    block_ids = jnp.arange(1024, dtype=jnp.int32)
    is_source = block_source[:, None] == block_ids[None, :]
    dest_block = jnp.sum(jnp.where(is_source, block_ids[:, None], 0), axis=0)
    dest_device = (dest_block // 32).reshape(32, 32)
    same_dest = dest_device[:, :, None] == dest_device[:, None, :]
    slot_ids = jnp.arange(32, dtype=jnp.int32)
    before = slot_ids[None, :] < slot_ids[:, None]
    rank = jnp.sum((same_dest & before[None]).astype(jnp.int32), axis=2)
    own_x = jnp.stack([x, (x + 3) % 4, (x + 1) % 4, (x + 2) % 4]).astype(jnp.int32)
    spread_ids = (own_x * NZ + z)[:, None, None] == slot_ids[None, :, None]
    dest_own = jnp.sum(jnp.where(spread_ids, dest_device[None], 0), axis=1)
    rank_own = jnp.sum(jnp.where(spread_ids, rank[None], 0), axis=1)
    lanes = (
        (dest_own // 4) * 128 + ((dest_own % 4 + own_x[:, None]) % 4) * 32 + rank_own * 16
    )
    lane_pos = (lanes[:, :, None] + jnp.arange(16, dtype=jnp.int32)).reshape(4, 512)
    source = lax.dynamic_slice_in_dim(block_source, dev * 32, 32)
    source_dev = source // 32
    source_rank = jnp.sum(
        jnp.where(block_ids[None, :] == source[:, None], rank.reshape(-1)[None, :], 0), axis=1
    )
    spot = (
        (source_dev % NZ) * 128 + ((dev % 4 + source_dev // NZ) % 4) * 32 + source_rank * 16
    )
    row_pos = (spot[:, None] + jnp.arange(16, dtype=jnp.int32)).reshape(1, 512)

    where = ((z - jnp.array([0, 1, 2, 3, 4, -1, -2, -3], jnp.int32)) % NZ).astype(jnp.int32)
    core = c.reshape(1).astype(jnp.int32)

    w0 = spread_columns(weight)
    s0 = move(rows, dc=1)
    gain_post = post_gain.astype(F32)[:, None]
    gain_final = final_gain.astype(F32)[:, None]
    out_value = mlp_out.T.astype(F32)
    sum_out = swap_rows(jnp.sum(out_value * out_value, axis=0)[None])
    w0, sum_out, where = lax.optimization_barrier((w0, sum_out, where))
    if W_FIRST:
        w0, rows = lax.optimization_barrier((w0, rows))
    r1, r2 = move(rows, dx=1), move(rows, dx=-1)
    if R3 == 0:
        r3 = move(rows, dx=2)
    f1, g1 = move(w0, dz=1), move(w0, dz=-1)
    f2, g2 = move(f1, dz=1), move(g1, dz=-1)
    f3, g3 = move(f2, dz=1), move(g2, dz=-1)
    if TIE:
        r1, r2, f3, g3, s0 = lax.optimization_barrier((r1, r2, f3, g3, s0))
    f4 = move(f3, dz=1)
    s1, s2 = move(r1, dc=1), move(r2, dc=1)
    if R3 == 0:
        s3 = move(r3, dc=1)
        far_rows, far_swapped = (r3,), (s3,)
    else:
        r3a, r3b = move(r1[:256], dx=1), move(r2[256:], dx=-1)
        s3a, s3b = move(r3a, dc=1), move(r3b, dc=1)
        far_rows, far_swapped = (r3a, r3b), (s3a, s3b)

    mid_value = hidden_mid.T.astype(F32)
    out_scale = lax.rsqrt(jnp.sum(sum_out, axis=0) / 3584 + EPS)
    gout = out_value * gain_post
    resid = mid_value + gout * out_scale
    pair = jnp.stack([jnp.sum(resid * resid, axis=0), jnp.sum(resid * gout, axis=0)])
    active, slope = gelu_parts(gate_pre.astype(F32))
    slope = slope * up_pre.astype(F32)
    down_share, r1 = lax.optimization_barrier((down_weight.T, r1))
    down = lax.all_gather(down_share, "dp", axis=0, tiled=True)

    pieces = (w0, f1, f2, f3, f4, g1, g2, g3)

    def part(left, right):
        size = sum(ref.shape[0] for ref in left)
        parts = call(
            part_kernel,
            jax.ShapeDtypeStruct((4, 112, size), BF),
            2,
            8 + 2 * len(left),
            2 * size * 448 * 2048,
            [
                pltpu.VMEM((2, 448, 1024), BF),
                pltpu.VMEM((2, size, 1024), BF),
                pltpu.SemaphoreType.DMA((8 + 2 * len(left),)),
            ],
            name="part",
            space=pl.ANY,
        )(where, core, *pieces, *left, *right)
        return lax.all_to_all(
            parts, "head", 0, 0, axis_index_groups=[[0, 2, 4, 6], [1, 3, 5, 7]], tiled=True
        )

    first = part((rows, r1, r2), (s0, s1, s2))
    last = part(far_rows, far_swapped)
    first, lane_pos, row_pos = lax.optimization_barrier((first, lane_pos, row_pos))
    outgoing = call(
        send_kernel,
        jax.ShapeDtypeStruct((32, 112, 128), BF),
        1,
        3,
        2 * 112 * 2048 * 1024,
        [pltpu.VMEM((4, 112, 1024), BF)],
        name="send",
    )(own_x, first, last, lane_pos)
    arrived = lax.all_to_all(outgoing, "dp", 0, 0, tiled=True)
    arrived, resid, gout, pair, out_scale, active, slope = lax.optimization_barrier(
        (arrived, resid, gout, pair, out_scale, active, slope)
    )
    norm_grad, dots = call(
        recv_kernel,
        (jax.ShapeDtypeStruct((448, 512), F32), jax.ShapeDtypeStruct((8, 4, 512), F32)),
        0,
        6,
        2 * 448 * 512 * 1024,
        name="recv",
    )(arrived, row_pos, resid, gout, gain_final, pair)
    dots = lax.all_to_all(dots, "head", 0, 0, tiled=True)
    resid_grad, post = call(
        norm_kernel,
        (jax.ShapeDtypeStruct((512, 448), BF), jax.ShapeDtypeStruct((448, 512), BF)),
        0,
        6,
        448 * 512 * 20,
        name="norm",
    )(norm_grad, resid, out_value, gain_post, out_scale, dots)
    p1, p2, p3 = move(post, dy=1), move(post, dy=-1), move(post, dy=2)
    q0 = move(post, dc=1)
    q1, q2, q3 = move(p1, dc=1), move(p2, dc=1), move(p3, dc=1)
    from_y = jnp.stack([y, y, y + 3, y + 3, y + 1, y + 1, y + 2, y + 2]) % 4
    from_c = (c + jnp.array([0, 1] * 4, jnp.int32)) % 2
    heads = (from_y * 2 + from_c).astype(jnp.int32)
    gate_grad, up_grad = call(
        final_kernel,
        (jax.ShapeDtypeStruct((512, 896), BF), jax.ShapeDtypeStruct((512, 896), BF)),
        1,
        11,
        2 * 512 * 896 * 3584,
        [
            pltpu.VMEM((8, 448, 512), BF),
            pltpu.VMEM((8, 448, 896), BF),
            pltpu.VMEM((2, 512, 896), F32),
            pltpu.SemaphoreType.DMA((18,)),
        ],
        name="final",
        space=pl.ANY,
    )(heads, post, q0, p1, q1, p2, q2, p3, q3, down, slope, active)
    return (resid_grad, gate_grad, up_grad)


def solution(mesh):
    return jax.shard_map(
        per_device,
        mesh=mesh,
        in_specs=(
            P(None, "dp", "head"),
            P(None, "dp", "head"),
            P(None, "dp", "head"),
            P(None, "dp", "head"),
            P(),
            P("dp", "head"),
            P("dp", "head"),
            P("head"),
            P("head"),
            P("dp", "head"),
            P("dp", "head"),
            P("head", "dp"),
        ),
        out_specs=(P("dp", "head"), P("dp", "head"), P("dp", "head")),
        check_vma=False,
    )
```

```python
import jax
import jax.numpy as jnp
from jax import lax
from jax.experimental import pallas as pl
from jax.experimental.pallas import tpu as pltpu
from jax.sharding import PartitionSpec as P

EPS = 1e-06
NX, NZ, NY, NC = 4, 8, 4, 2
AXES = ("dp", "head")
BF = jnp.bfloat16
F32 = jnp.float32
MIB = 56
W_FIRST = 0
R3 = 1
TIE = 2
SPLIT = 2
DOTS = 1


def move(value, dx=0, dz=0, dy=0, dc=0):
    pairs = []
    for x in range(NX):
        for z in range(NZ):
            for y in range(NY):
                for c in range(NC):
                    src = (x * NZ + z) * 8 + y * NC + c
                    dst = (
                        ((x + dx) % NX * NZ + (z + dz) % NZ) * 8
                        + (y + dy) % NY * NC
                        + (c + dc) % NC
                    )
                    pairs.append((src, dst))
    return lax.ppermute(value, AXES, pairs)


def spread_columns(shard):
    pairs = []
    for x in range(NX):
        for z in range(NZ):
            for y in range(NY):
                for c in range(NC):
                    d, t = z // 4, z % 4
                    src = (x * NZ + z) * 8 + y * NC + c
                    pairs.append((src, (t * NZ + 4 * c + x) * 8 + y * NC + d))
    return lax.ppermute(shard, AXES, pairs)


def call(kernel, out_shape, n_scalar, n_array, flops, scratch=(), name=None, space=pltpu.VMEM):
    return pl.pallas_call(
        kernel,
        out_shape=out_shape,
        in_specs=[pl.BlockSpec(memory_space=pltpu.SMEM)] * n_scalar
        + [pl.BlockSpec(memory_space=space)] * n_array,
        out_specs=jax.tree.map(lambda _: pl.BlockSpec(memory_space=pltpu.VMEM), out_shape),
        scratch_shapes=scratch,
        compiler_params=pltpu.CompilerParams(vmem_limit_bytes=MIB * 1024 * 1024),
        cost_estimate=pl.CostEstimate(flops=flops, bytes_accessed=6_000_000, transcendentals=0),
        name=name,
    )


def dot_nt(a, b):
    return lax.dot_general(a, b, (((1,), (1,)), ((), ())), preferred_element_type=F32)


def dot_tn(a, b):
    return lax.dot_general(a, b, (((0,), (0,)), ((), ())), preferred_element_type=F32)


def part_kernel(where, core, *refs):
    pieces, out, wall, rows, sems = refs[:8], refs[-4], refs[-3], refs[-2], refs[-1]
    count = (len(refs) - 12) // 2
    copies = []
    for k, ref in enumerate(pieces):
        at = pl.multiple_of(where[k] % 4 * 112, 16)
        spot = wall.at[where[k] // 4, pl.ds(at, 112)]
        copies.append(pltpu.make_async_copy(ref, spot, sems.at[k]))
    at = 0
    for k in range(count):
        size = refs[8 + k].shape[0]
        for side in range(2):
            spot = rows.at[side, pl.ds(at, size)]
            ref, sem = refs[8 + side * count + k], sems.at[8 + 2 * k + side]
            copies.append(pltpu.make_async_copy(ref, spot, sem))
        at += size
    for copy in copies:
        copy.start()
    for copy in copies[:8]:
        copy.wait()
    own, other = wall[core[0]], wall[1 - core[0]]
    at = 0
    for k in range(count):
        size = refs[8 + k].shape[0]
        copies[8 + 2 * k].wait()
        copies[9 + 2 * k].wait()
        prod = dot_nt(own, rows[0, at : at + size, :])
        prod = (prod + dot_nt(other, rows[1, at : at + size, :])).astype(BF)
        for y in range(4):
            out[y, :, at : at + size] = prod[y * 112 : (y + 1) * 112, :]
        at += size


def send_kernel(xs, *refs):
    groups, (lane_pos, out, moved) = refs[:-3], refs[-3:]
    blocks = [(ref, at) for ref in groups for at in range(0, ref.shape[2], 512)]
    for r, (parts, at) in enumerate(blocks):
        total = parts[0, :, at : at + 512].astype(F32)
        for g in range(1, 4):
            total = total + parts[g, :, at : at + 512].astype(F32)
        ids = lax.broadcasted_iota(jnp.int32, (1024, 512), 0)
        pick = jnp.where(ids == lane_pos[r : r + 1, :], 1.0, 0.0).astype(BF)
        moved[xs[r]] = dot_nt(total.astype(BF), pick).astype(BF)
    group = lax.broadcasted_iota(jnp.int32, (112, 128), 1) // 32
    for q in range(8):
        tiles = [moved[x, :, q * 128 : (q + 1) * 128] for x in range(4)]
        for j in range(4):
            here = tiles[(0 - j) % 4]
            for g in range(1, 4):
                here = jnp.where(group == g, tiles[(g - j) % 4], here)
            out[4 * q + j] = here


def stats_kernel(bundle, stats, held, sems):
    copies = []
    for k in range(8):
        rows = bundle.at[pl.ds(k * 912, 912)]
        copies.append(pltpu.make_async_copy(rows, held.at[k], sems.at[k]))
    for copy in copies:
        copy.start()
    total = jnp.zeros((1, 512), F32)
    for k in range(8):
        copies[k].wait()
        value = held[k, 448:896, :].astype(F32)
        total = total + jnp.sum(value * value, axis=0, keepdims=True)
    out_scale = lax.rsqrt(total / 3584.0 + EPS)
    square = jnp.zeros((1, 512), F32)
    cross = jnp.zeros((1, 512), F32)
    for k in range(8):
        gain = held[k, 896:912, :].astype(F32).T[:448, 0:1]
        gout = held[k, 448:896, :].astype(F32) * gain
        resid = held[k, 0:448, :].astype(F32) + gout * out_scale
        square = square + jnp.sum(resid * resid, axis=0, keepdims=True)
        cross = cross + jnp.sum(resid * gout, axis=0, keepdims=True)
    stats[...] = jnp.concatenate(
        [out_scale, lax.rsqrt(square / 3584.0 + EPS), cross, jnp.zeros((5, 512), F32)], axis=0
    )


def recv_kernel(arrived, row_pos, mid, out, gain_post, gain_final, stats, grad, dots):
    ids = lax.broadcasted_iota(jnp.int32, (1024, 512), 0)
    pick = jnp.where(ids == row_pos[...], 1.0, 0.0).astype(BF)
    out_scale = stats[0:1, :]
    first = jnp.zeros((1, 512), F32)
    second = jnp.zeros((1, 512), F32)
    for x in range(4):
        side = jnp.concatenate([arrived[x * 8 + z] for z in range(8)], axis=1)
        rows = slice(x * 112, (x + 1) * 112)
        piece = jnp.dot(side, pick, preferred_element_type=F32)
        grad[rows, :] = piece.astype(BF)
        piece = piece * gain_final[rows, :]
        gout = out[rows, :].astype(F32) * gain_post[rows, :]
        resid = mid[rows, :].astype(F32) + gout * out_scale
        first = first + jnp.sum(piece * resid, axis=0, keepdims=True)
        second = second + jnp.sum(piece * gout, axis=0, keepdims=True)
    for k in range(8):
        dots[k, 0:1, :] = first
        dots[k, 1:2, :] = second


def row_factors(stats, dots):
    sums = dots[0]
    for k in range(1, 8):
        sums = sums + dots[k]
    out_scale, resid_scale, cross = stats[0:1, :], stats[1:2, :], stats[2:3, :]
    final_mean = resid_scale * sums[0:1, :] / 3584.0
    post_dot = resid_scale * (sums[1:2, :] - resid_scale * final_mean * cross)
    post_mean = out_scale * post_dot / 3584.0
    return out_scale, resid_scale, resid_scale * final_mean, out_scale * post_mean


def resid_kernel(grad, mid, out, gain_post, gain_final, stats, dots, resid_grad):
    out_scale, resid_scale, pull, _ = row_factors(stats, dots)
    norm_grad = grad[...].astype(F32) * gain_final[...]
    resid = mid[...].astype(F32) + out[...].astype(F32) * gain_post[...] * out_scale
    resid_grad[...] = (resid_scale * (norm_grad - resid * pull)).astype(BF)


def final_kernel(heads, *refs):
    grads, (weight, bundle, slope, active, stats, dots, gate, up) = refs[:8], refs[8:16]
    grad_buf, weight_buf, held, scale_buf, stat_buf, dot_buf, sems = refs[16:]
    copies = [
        pltpu.make_async_copy(stats, stat_buf, sems.at[26]),
        pltpu.make_async_copy(dots, dot_buf, sems.at[27]),
    ]
    for k in range(8):
        at = pl.multiple_of(heads[k] * 448, 64)
        start = pl.multiple_of(heads[k] * 912, 16)
        copies.append(pltpu.make_async_copy(grads[k], grad_buf.at[k], sems.at[3 * k]))
        rows = bundle.at[pl.ds(start, 912)]
        copies.append(pltpu.make_async_copy(rows, held.at[k], sems.at[3 * k + 1]))
        rows = weight.at[pl.ds(at, 448)]
        copies.append(pltpu.make_async_copy(rows, weight_buf.at[k], sems.at[3 * k + 2]))
    copies.append(pltpu.make_async_copy(slope, scale_buf.at[0], sems.at[24]))
    copies.append(pltpu.make_async_copy(active, scale_buf.at[1], sems.at[25]))
    for copy in copies:
        copy.start()
    copies[0].wait()
    copies[1].wait()
    out_scale, resid_scale, pull, push = row_factors(stat_buf, dot_buf)
    value = jnp.zeros((512, 896), F32)
    for k in range(8):
        for copy in copies[2 + 3 * k : 5 + 3 * k]:
            copy.wait()
        gains = held[k, 896:912, :].astype(F32).T
        gain_post, gain_final = gains[:448, 0:1], gains[:448, 1:2]
        out = held[k, 448:896, :].astype(F32)
        resid = held[k, 0:448, :].astype(F32) + out * gain_post * out_scale
        total = resid_scale * (grad_buf[k].astype(F32) * gain_final - resid * pull)
        post = out_scale * (total * gain_post - out * push)
        value = value + dot_tn(post.astype(BF), weight_buf[k])
    copies[26].wait()
    copies[27].wait()
    gate[...] = (value * scale_buf[0]).astype(BF)
    up[...] = (value * scale_buf[1]).astype(BF)


def gelu_parts(gate_value):
    activated, pullback = jax.vjp(
        lambda pre_act: jax.nn.gelu(pre_act, approximate=True), gate_value
    )
    return (activated, pullback(jnp.ones_like(gate_value))[0])


def per_device(
    key_grads,
    value_grads,
    key_weight,
    value_weight,
    block_source,
    hidden_mid,
    mlp_out,
    post_gain,
    final_gain,
    gate_pre,
    up_pre,
    down_weight,
):
    dev = lax.axis_index("dp")
    head = lax.axis_index("head")
    x, z = dev // NZ, dev % NZ
    y, c = head // NC, head % NC

    weight = jnp.concatenate([key_weight[0], key_weight[1], value_weight[0], value_weight[1]], 1)
    rows = jnp.concatenate([key_grads[0], key_grads[1], value_grads[0], value_grads[1]], 1)
    block_ids = jnp.arange(1024, dtype=jnp.int32)
    is_source = block_source[:, None] == block_ids[None, :]
    dest_block = jnp.sum(jnp.where(is_source, block_ids[:, None], 0), axis=0)
    dest_device = (dest_block // 32).reshape(32, 32)
    same_dest = dest_device[:, :, None] == dest_device[:, None, :]
    slot_ids = jnp.arange(32, dtype=jnp.int32)
    before = slot_ids[None, :] < slot_ids[:, None]
    rank = jnp.sum((same_dest & before[None]).astype(jnp.int32), axis=2)
    own_x = jnp.stack([x, (x + 3) % 4, (x + 1) % 4, (x + 2) % 4]).astype(jnp.int32)
    spread_ids = (own_x * NZ + z)[:, None, None] == slot_ids[None, :, None]
    dest_own = jnp.sum(jnp.where(spread_ids, dest_device[None], 0), axis=1)
    rank_own = jnp.sum(jnp.where(spread_ids, rank[None], 0), axis=1)
    lanes = (
        (dest_own // 4) * 128 + ((dest_own % 4 + own_x[:, None]) % 4) * 32 + rank_own * 16
    )
    lane_pos = (lanes[:, :, None] + jnp.arange(16, dtype=jnp.int32)).reshape(4, 512)
    source = lax.dynamic_slice_in_dim(block_source, dev * 32, 32)
    source_dev = source // 32
    source_rank = jnp.sum(
        jnp.where(block_ids[None, :] == source[:, None], rank.reshape(-1)[None, :], 0), axis=1
    )
    spot = (
        (source_dev % NZ) * 128 + ((dev % 4 + source_dev // NZ) % 4) * 32 + source_rank * 16
    )
    row_pos = (spot[:, None] + jnp.arange(16, dtype=jnp.int32)).reshape(1, 512)

    where = ((z - jnp.array([0, 1, 2, 3, 4, -1, -2, -3], jnp.int32)) % NZ).astype(jnp.int32)
    core = c.reshape(1).astype(jnp.int32)

    w0 = spread_columns(weight)
    s0 = move(rows, dc=1)
    gains = jnp.pad(jnp.stack([post_gain, final_gain]), ((0, 14), (0, 64)))
    bundle = jnp.concatenate([hidden_mid.T, mlp_out.T, gains], axis=0)
    bundle = lax.all_gather(bundle, "head", axis=0, tiled=True)
    w0, where = lax.optimization_barrier((w0, where))
    if W_FIRST:
        w0, rows = lax.optimization_barrier((w0, rows))
    r1, r2 = move(rows, dx=1), move(rows, dx=-1)
    if R3 == 0:
        r3 = move(rows, dx=2)
    f1, g1 = move(w0, dz=1), move(w0, dz=-1)
    f2, g2 = move(f1, dz=1), move(g1, dz=-1)
    if TIE == 2:
        r1, r2, f2, g2, s0 = lax.optimization_barrier((r1, r2, f2, g2, s0))
    f3, g3 = move(f2, dz=1), move(g2, dz=-1)
    if TIE == 1:
        r1, r2, f3, g3, s0 = lax.optimization_barrier((r1, r2, f3, g3, s0))
    f4 = move(f3, dz=1)
    s1, s2 = move(r1, dc=1), move(r2, dc=1)
    if R3 == 0:
        s3 = move(r3, dc=1)
        far_rows, far_swapped = (r3,), (s3,)
    else:
        r3a, r3b = move(r1[:256], dx=1), move(r2[256:], dx=-1)
        s3a, s3b = move(r3a, dc=1), move(r3b, dc=1)
        far_rows, far_swapped = (r3a, r3b), (s3a, s3b)

    gain_post = post_gain.astype(F32)[:, None]
    gain_final = final_gain.astype(F32)[:, None]
    active, slope = gelu_parts(gate_pre.astype(F32))
    slope = slope * up_pre.astype(F32)
    down_share, r1 = lax.optimization_barrier((down_weight.T, r1))
    down = lax.all_gather(down_share, "dp", axis=0, tiled=True)

    pieces = (w0, f1, f2, f3, f4, g1, g2, g3)

    def part(left, right):
        size = sum(ref.shape[0] for ref in left)
        parts = call(
            part_kernel,
            jax.ShapeDtypeStruct((4, 112, size), BF),
            2,
            8 + 2 * len(left),
            2 * size * 448 * 2048,
            [
                pltpu.VMEM((2, 448, 1024), BF),
                pltpu.VMEM((2, size, 1024), BF),
                pltpu.SemaphoreType.DMA((8 + 2 * len(left),)),
            ],
            name="part",
            space=pl.ANY,
        )(where, core, *pieces, *left, *right)
        return lax.all_to_all(
            parts, "head", 0, 0, axis_index_groups=[[0, 2, 4, 6], [1, 3, 5, 7]], tiled=True
        )

    if SPLIT == 2:
        groups = [part((rows, r1, r2), (s0, s1, s2))]
    else:
        groups = [part((rows,), (s0,)), part((r1, r2), (s1, s2))]
    groups.append(part(far_rows, far_swapped))
    groups[0], lane_pos, row_pos = lax.optimization_barrier((groups[0], lane_pos, row_pos))
    outgoing = call(
        send_kernel,
        jax.ShapeDtypeStruct((32, 112, 128), BF),
        1,
        len(groups) + 1,
        2 * 112 * 2048 * 1024,
        [pltpu.VMEM((4, 112, 1024), BF)],
        name="send",
    )(own_x, *groups, lane_pos)
    arrived = lax.all_to_all(outgoing, "dp", 0, 0, tiled=True)
    stats = call(
        stats_kernel,
        jax.ShapeDtypeStruct((8, 512), F32),
        0,
        1,
        3584 * 512 * 12,
        [pltpu.VMEM((8, 912, 512), BF), pltpu.SemaphoreType.DMA((8,))],
        name="stats",
        space=pl.ANY,
    )(bundle)
    arrived, stats, active, slope = lax.optimization_barrier((arrived, stats, active, slope))
    mid, out = hidden_mid.T, mlp_out.T
    grad, dots = call(
        recv_kernel,
        (jax.ShapeDtypeStruct((448, 512), BF), jax.ShapeDtypeStruct((8, 2, 512), F32)),
        0,
        7,
        2 * 448 * 512 * 1024,
        name="recv",
    )(arrived, row_pos, mid, out, gain_post, gain_final, stats)
    p1, p2, p3 = move(grad, dy=1), move(grad, dy=-1), move(grad, dy=2)
    q0 = move(grad, dc=1)
    dots = lax.all_to_all(dots, "head", 0, 0, tiled=True)
    if DOTS:
        p1, p2, p3, dots = lax.optimization_barrier((p1, p2, p3, dots))
    q1, q2, q3 = move(p1, dc=1), move(p2, dc=1), move(p3, dc=1)
    resid_grad = call(
        resid_kernel,
        jax.ShapeDtypeStruct((448, 512), BF),
        0,
        7,
        448 * 512 * 20,
        name="resid",
    )(grad, mid, out, gain_post, gain_final, stats, dots)
    from_y = jnp.stack([y, y, y + 3, y + 3, y + 1, y + 1, y + 2, y + 2]) % 4
    from_c = (c + jnp.array([0, 1] * 4, jnp.int32)) % 2
    heads = (from_y * 2 + from_c).astype(jnp.int32)
    gate_grad, up_grad = call(
        final_kernel,
        (jax.ShapeDtypeStruct((512, 896), BF), jax.ShapeDtypeStruct((512, 896), BF)),
        1,
        14,
        2 * 512 * 896 * 3584,
        [
            pltpu.VMEM((8, 448, 512), BF),
            pltpu.VMEM((8, 448, 896), BF),
            pltpu.VMEM((8, 912, 512), BF),
            pltpu.VMEM((2, 512, 896), F32),
            pltpu.VMEM((8, 512), F32),
            pltpu.VMEM((8, 2, 512), F32),
            pltpu.SemaphoreType.DMA((28,)),
        ],
        name="final",
        space=pl.ANY,
    )(heads, grad, q0, p1, q1, p2, q2, p3, q3, down, bundle, slope, active, stats, dots)
    return (resid_grad.T, gate_grad, up_grad)


def solution(mesh):
    return jax.shard_map(
        per_device,
        mesh=mesh,
        in_specs=(
            P(None, "dp", "head"),
            P(None, "dp", "head"),
            P(None, "dp", "head"),
            P(None, "dp", "head"),
            P(),
            P("dp", "head"),
            P("dp", "head"),
            P("head"),
            P("head"),
            P("dp", "head"),
            P("dp", "head"),
            P("head", "dp"),
        ),
        out_specs=(P("dp", "head"), P("dp", "head"), P("dp", "head")),
        check_vma=False,
    )
```

```python
import jax
import jax.numpy as jnp
from jax import lax
from jax.experimental import pallas as pl
from jax.experimental.pallas import tpu as pltpu
from jax.sharding import PartitionSpec as P

EPS = 1e-06
NX, NZ, NY, NC = 4, 8, 4, 2
AXES = ("dp", "head")
BF = jnp.bfloat16
F32 = jnp.float32
MIB = 56


def move(value, dx=0, dz=0, dy=0, dc=0):
    pairs = []
    for x in range(NX):
        for z in range(NZ):
            for y in range(NY):
                for c in range(NC):
                    src = (x * NZ + z) * 8 + y * NC + c
                    dst = (
                        ((x + dx) % NX * NZ + (z + dz) % NZ) * 8
                        + (y + dy) % NY * NC
                        + (c + dc) % NC
                    )
                    pairs.append((src, dst))
    return lax.ppermute(value, AXES, pairs)


def spread_columns(shard):
    pairs = []
    for x in range(NX):
        for z in range(NZ):
            for y in range(NY):
                for c in range(NC):
                    d, t = z // 4, z % 4
                    src = (x * NZ + z) * 8 + y * NC + c
                    pairs.append((src, (t * NZ + 4 * c + x) * 8 + y * NC + d))
    return lax.ppermute(shard, AXES, pairs)


def call(kernel, out_shape, n_scalar, n_array, flops, scratch=(), name=None, space=pltpu.VMEM):
    return pl.pallas_call(
        kernel,
        out_shape=out_shape,
        in_specs=[pl.BlockSpec(memory_space=pltpu.SMEM)] * n_scalar
        + [pl.BlockSpec(memory_space=space)] * n_array,
        out_specs=jax.tree.map(lambda _: pl.BlockSpec(memory_space=pltpu.VMEM), out_shape),
        scratch_shapes=scratch,
        compiler_params=pltpu.CompilerParams(vmem_limit_bytes=MIB * 1024 * 1024),
        cost_estimate=pl.CostEstimate(flops=flops, bytes_accessed=6_000_000, transcendentals=0),
        name=name,
    )


def dot_nt(a, b):
    return lax.dot_general(a, b, (((1,), (1,)), ((), ())), preferred_element_type=F32)


def dot_tn(a, b):
    return lax.dot_general(a, b, (((0,), (0,)), ((), ())), preferred_element_type=F32)


def part_kernel(where, core, *refs):
    pieces, outs, (wall, rows, sems) = refs[:8], refs[-7:-3], refs[-3:]
    count = (len(refs) - 15) // 2
    copies = []
    for k, ref in enumerate(pieces):
        at = pl.multiple_of(where[k] % 4 * 112, 16)
        spot = wall.at[where[k] // 4, pl.ds(at, 112)]
        copies.append(pltpu.make_async_copy(ref, spot, sems.at[k]))
    at = 0
    for k in range(count):
        size = refs[8 + k].shape[0]
        for side in range(2):
            spot = rows.at[side, pl.ds(at, size)]
            ref, sem = refs[8 + side * count + k], sems.at[8 + 2 * k + side]
            copies.append(pltpu.make_async_copy(ref, spot, sem))
        at += size
    for copy in copies:
        copy.start()
    for copy in copies[:8]:
        copy.wait()
    own, other = wall[core[0]], wall[1 - core[0]]
    at = 0
    for k in range(count):
        size = refs[8 + k].shape[0]
        copies[8 + 2 * k].wait()
        copies[9 + 2 * k].wait()
        prod = dot_nt(own, rows[0, at : at + size, :])
        prod = (prod + dot_nt(other, rows[1, at : at + size, :])).astype(BF)
        for k in range(4):
            outs[k][:, at : at + size] = prod[k * 112 : (k + 1) * 112, :]
        at += size


def send_kernel(xs, *refs):
    first, last, (lane_pos, out, moved) = refs[:4], refs[4:8], refs[8:]
    for r in range(4):
        parts, at = (first, r * 512) if r < 3 else (last, 0)
        total = parts[0][:, at : at + 512].astype(F32)
        for part in parts[1:]:
            total = total + part[:, at : at + 512].astype(F32)
        ids = lax.broadcasted_iota(jnp.int32, (1024, 512), 0)
        pick = jnp.where(ids == lane_pos[r : r + 1, :], 1.0, 0.0).astype(BF)
        moved[xs[r]] = dot_nt(total.astype(BF), pick).astype(BF)
    group = lax.broadcasted_iota(jnp.int32, (112, 128), 1) // 32
    for q in range(8):
        tiles = [moved[x, :, q * 128 : (q + 1) * 128] for x in range(4)]
        for j in range(4):
            here = tiles[(0 - j) % 4]
            for g in range(1, 4):
                here = jnp.where(group == g, tiles[(g - j) % 4], here)
            out[4 * q + j] = here


def stats_kernel(bundle, stats, held, sems):
    copies = []
    for k in range(8):
        rows = bundle.at[pl.ds(k * 912, 912)]
        copies.append(pltpu.make_async_copy(rows, held.at[k], sems.at[k]))
    for copy in copies:
        copy.start()
    total = jnp.zeros((1, 512), F32)
    for k in range(8):
        copies[k].wait()
        value = held[k, 448:896, :].astype(F32)
        total = total + jnp.sum(value * value, axis=0, keepdims=True)
    out_scale = lax.rsqrt(total / 3584.0 + EPS)
    square = jnp.zeros((1, 512), F32)
    cross = jnp.zeros((1, 512), F32)
    for k in range(8):
        gain = held[k, 896:912, :].astype(F32).T[:448, 0:1]
        gout = held[k, 448:896, :].astype(F32) * gain
        resid = held[k, 0:448, :].astype(F32) + gout * out_scale
        square = square + jnp.sum(resid * resid, axis=0, keepdims=True)
        cross = cross + jnp.sum(resid * gout, axis=0, keepdims=True)
    stats[...] = jnp.concatenate(
        [out_scale, lax.rsqrt(square / 3584.0 + EPS), cross, jnp.zeros((5, 512), F32)], axis=0
    )


def recv_kernel(arrived, row_pos, mid, out, gain_post, gain_final, stats, grad):
    ids = lax.broadcasted_iota(jnp.int32, (1024, 512), 0)
    pick = jnp.where(ids == row_pos[...], 1.0, 0.0).astype(BF)
    out_scale = stats[0:1, :]
    first = jnp.zeros((1, 512), F32)
    second = jnp.zeros((1, 512), F32)
    for x in range(4):
        side = jnp.concatenate([arrived[x * 8 + z] for z in range(8)], axis=1)
        rows = slice(x * 112, (x + 1) * 112)
        piece = jnp.dot(side, pick, preferred_element_type=F32)
        grad[rows, :] = piece.astype(BF)
        piece = piece * gain_final[rows, :]
        gout = out[rows, :].astype(F32) * gain_post[rows, :]
        resid = mid[rows, :].astype(F32) + gout * out_scale
        first = first + jnp.sum(piece * resid, axis=0, keepdims=True)
        second = second + jnp.sum(piece * gout, axis=0, keepdims=True)
    parts = []
    for value in (first, second):
        for _ in range(3):
            parts.append(value.astype(BF).astype(F32))
            value = value - parts[-1]
    parts.append(jnp.zeros((10, 512), F32))
    grad[448:464, :] = jnp.concatenate(parts, axis=0).astype(BF)


def row_factors(stats, grads):
    sums = grads[0, 448:464, :].astype(F32)
    for k in range(1, 8):
        sums = sums + grads[k, 448:464, :].astype(F32)
    first = sums[0:1, :] + sums[1:2, :] + sums[2:3, :]
    second = sums[3:4, :] + sums[4:5, :] + sums[5:6, :]
    out_scale, resid_scale, cross = stats[0:1, :], stats[1:2, :], stats[2:3, :]
    final_mean = resid_scale * first / 3584.0
    post_dot = resid_scale * (second - resid_scale * final_mean * cross)
    post_mean = out_scale * post_dot / 3584.0
    return out_scale, resid_scale, resid_scale * final_mean, out_scale * post_mean


def final_kernel(heads, *refs):
    grads, (weight, bundle, slope, active, stats, resid_grad, gate, up) = refs[:8], refs[8:16]
    grad_buf, weight_buf, held, scale_buf, stat_buf, sems = refs[16:]
    copies = [pltpu.make_async_copy(stats, stat_buf, sems.at[26])]
    for k in range(8):
        copies.append(pltpu.make_async_copy(grads[k], grad_buf.at[k], sems.at[3 * k]))
    for k in range(8):
        at = pl.multiple_of(heads[k] * 448, 64)
        start = pl.multiple_of(heads[k] * 912, 16)
        rows = bundle.at[pl.ds(start, 912)]
        copies.append(pltpu.make_async_copy(rows, held.at[k], sems.at[3 * k + 1]))
        rows = weight.at[pl.ds(at, 448)]
        copies.append(pltpu.make_async_copy(rows, weight_buf.at[k], sems.at[3 * k + 2]))
    copies.append(pltpu.make_async_copy(slope, scale_buf.at[0], sems.at[24]))
    copies.append(pltpu.make_async_copy(active, scale_buf.at[1], sems.at[25]))
    for copy in copies:
        copy.start()
    for copy in copies[:9]:
        copy.wait()
    out_scale, resid_scale, pull, push = row_factors(stat_buf, grad_buf)
    value = jnp.zeros((512, 896), F32)
    for k in range(8):
        for copy in copies[9 + 2 * k : 11 + 2 * k]:
            copy.wait()
        gains = held[k, 896:912, :].astype(F32).T
        gain_post, gain_final = gains[:448, 0:1], gains[:448, 1:2]
        out = held[k, 448:896, :].astype(F32)
        resid = held[k, 0:448, :].astype(F32) + out * gain_post * out_scale
        norm_grad = grad_buf[k, 0:448, :].astype(F32) * gain_final
        total = resid_scale * (norm_grad - resid * pull)
        if k == 0:
            resid_grad[...] = total.astype(BF)
        post = out_scale * (total * gain_post - out * push)
        value = value + dot_tn(post.astype(BF), weight_buf[k])
    for copy in copies[25:]:
        copy.wait()
    gate[...] = (value * scale_buf[0]).astype(BF)
    up[...] = (value * scale_buf[1]).astype(BF)


def gelu_parts(gate_value):
    activated, pullback = jax.vjp(
        lambda pre_act: jax.nn.gelu(pre_act, approximate=True), gate_value
    )
    return (activated, pullback(jnp.ones_like(gate_value))[0])


def per_device(
    key_grads,
    value_grads,
    key_weight,
    value_weight,
    block_source,
    hidden_mid,
    mlp_out,
    post_gain,
    final_gain,
    gate_pre,
    up_pre,
    down_weight,
):
    dev = lax.axis_index("dp")
    head = lax.axis_index("head")
    x, z = dev // NZ, dev % NZ
    y, c = head // NC, head % NC

    weight = jnp.concatenate([key_weight[0], key_weight[1], value_weight[0], value_weight[1]], 1)
    weight, key_grads, value_grads = lax.optimization_barrier((weight, key_grads, value_grads))
    rows = jnp.concatenate([key_grads[0], key_grads[1], value_grads[0], value_grads[1]], 1)
    block_ids = jnp.arange(1024, dtype=jnp.int32)
    is_source = block_source[:, None] == block_ids[None, :]
    dest_block = jnp.sum(jnp.where(is_source, block_ids[:, None], 0), axis=0)
    dest_device = (dest_block // 32).reshape(32, 32)
    same_dest = dest_device[:, :, None] == dest_device[:, None, :]
    slot_ids = jnp.arange(32, dtype=jnp.int32)
    before = slot_ids[None, :] < slot_ids[:, None]
    rank = jnp.sum((same_dest & before[None]).astype(jnp.int32), axis=2)
    own_x = jnp.stack([x, (x + 3) % 4, (x + 1) % 4, (x + 2) % 4]).astype(jnp.int32)
    spread_ids = (own_x * NZ + z)[:, None, None] == slot_ids[None, :, None]
    dest_own = jnp.sum(jnp.where(spread_ids, dest_device[None], 0), axis=1)
    rank_own = jnp.sum(jnp.where(spread_ids, rank[None], 0), axis=1)
    lanes = (
        (dest_own // 4) * 128 + ((dest_own % 4 + own_x[:, None]) % 4) * 32 + rank_own * 16
    )
    lane_pos = (lanes[:, :, None] + jnp.arange(16, dtype=jnp.int32)).reshape(4, 512)
    source = lax.dynamic_slice_in_dim(block_source, dev * 32, 32)
    source_dev = source // 32
    source_rank = jnp.sum(
        jnp.where(block_ids[None, :] == source[:, None], rank.reshape(-1)[None, :], 0), axis=1
    )
    spot = (
        (source_dev % NZ) * 128 + ((dev % 4 + source_dev // NZ) % 4) * 32 + source_rank * 16
    )
    row_pos = (spot[:, None] + jnp.arange(16, dtype=jnp.int32)).reshape(1, 512)

    where = ((z - jnp.array([0, 1, 2, 3, 4, -1, -2, -3], jnp.int32)) % NZ).astype(jnp.int32)
    core = c.reshape(1).astype(jnp.int32)

    w0 = spread_columns(weight)
    s0 = move(rows, dc=1)
    gains = jnp.pad(jnp.stack([post_gain, final_gain]), ((0, 14), (0, 64)))
    bundle = jnp.concatenate([hidden_mid.T, mlp_out.T, gains], axis=0)
    bundle = lax.all_gather(bundle, "head", axis=0, tiled=True)
    w0, where = lax.optimization_barrier((w0, where))
    r1, r2 = move(rows, dx=1), move(rows, dx=-1)
    f1, g1 = move(w0, dz=1), move(w0, dz=-1)
    f2, g2 = move(f1, dz=1), move(g1, dz=-1)
    r1, r2, f2, g2, s0 = lax.optimization_barrier((r1, r2, f2, g2, s0))
    f3, g3 = move(f2, dz=1), move(g2, dz=-1)
    f4 = move(f3, dz=1)
    s1, s2 = move(r1, dc=1), move(r2, dc=1)
    r3 = move(r1, dx=1)

    gain_post = post_gain.astype(F32)[:, None]
    gain_final = final_gain.astype(F32)[:, None]
    active, slope = gelu_parts(gate_pre.astype(F32))
    slope = slope * up_pre.astype(F32)
    down_share, r1 = lax.optimization_barrier((down_weight.T, r1))
    down = lax.all_gather(down_share, "dp", axis=0, tiled=True)

    pieces = (w0, f1, f2, f3, f4, g1, g2, g3)

    place = (where // 4 * 4 + (where % 4 - y) % NY).astype(jnp.int32)

    def part(left, right):
        size = sum(ref.shape[0] for ref in left)
        parts = call(
            part_kernel,
            (jax.ShapeDtypeStruct((112, size), BF),) * 4,
            2,
            8 + 2 * len(left),
            2 * size * 448 * 2048,
            [
                pltpu.VMEM((2, 448, 1024), BF),
                pltpu.VMEM((2, size, 1024), BF),
                pltpu.SemaphoreType.DMA((8 + 2 * len(left),)),
            ],
            name="part",
            space=pl.ANY,
        )(place, core, *pieces, *left, *right)
        return parts

    def over_y(parts):
        return [parts[0]] + [move(parts[k], dy=k) for k in (2, 1, 3)]

    first = part((rows, r1, r2), (s0, s1, s2))
    first, r3 = lax.optimization_barrier((first, r3))
    last = part((r3,), (move(r3, dc=1),))
    groups = over_y(first) + over_y(last)
    groups[0], lane_pos, row_pos = lax.optimization_barrier((groups[0], lane_pos, row_pos))
    outgoing = call(
        send_kernel,
        jax.ShapeDtypeStruct((32, 112, 128), BF),
        1,
        len(groups) + 1,
        2 * 112 * 2048 * 1024,
        [pltpu.VMEM((4, 112, 1024), BF)],
        name="send",
    )(own_x, *groups, lane_pos)
    arrived = lax.all_to_all(outgoing, "dp", 0, 0, tiled=True)
    stats = call(
        stats_kernel,
        jax.ShapeDtypeStruct((8, 512), F32),
        0,
        1,
        3584 * 512 * 12,
        [pltpu.VMEM((8, 912, 512), BF), pltpu.SemaphoreType.DMA((8,))],
        name="stats",
        space=pl.ANY,
    )(bundle)
    arrived, stats, active, slope = lax.optimization_barrier((arrived, stats, active, slope))
    mid, out = hidden_mid.T, mlp_out.T
    grad = call(
        recv_kernel,
        jax.ShapeDtypeStruct((464, 512), BF),
        0,
        7,
        2 * 448 * 512 * 1024,
        name="recv",
    )(arrived, row_pos, mid, out, gain_post, gain_final, stats)
    p1, p2, p3 = move(grad, dy=1), move(grad, dy=-1), move(grad, dy=2)
    q0 = move(grad, dc=1)
    q1, q2, q3 = move(p1, dc=1), move(p2, dc=1), move(p3, dc=1)
    from_y = jnp.stack([y, y, y + 3, y + 3, y + 1, y + 1, y + 2, y + 2]) % 4
    from_c = (c + jnp.array([0, 1] * 4, jnp.int32)) % 2
    heads = (from_y * 2 + from_c).astype(jnp.int32)
    resid_grad, gate_grad, up_grad = call(
        final_kernel,
        (
            jax.ShapeDtypeStruct((448, 512), BF),
            jax.ShapeDtypeStruct((512, 896), BF),
            jax.ShapeDtypeStruct((512, 896), BF),
        ),
        1,
        13,
        2 * 512 * 896 * 3584,
        [
            pltpu.VMEM((8, 464, 512), BF),
            pltpu.VMEM((8, 448, 896), BF),
            pltpu.VMEM((8, 912, 512), BF),
            pltpu.VMEM((2, 512, 896), F32),
            pltpu.VMEM((8, 512), F32),
            pltpu.SemaphoreType.DMA((27,)),
        ],
        name="final",
        space=pl.ANY,
    )(heads, grad, q0, p1, q1, p2, q2, p3, q3, down, bundle, slope, active, stats)
    return (resid_grad.T, gate_grad, up_grad)


def solution(mesh):
    return jax.shard_map(
        per_device,
        mesh=mesh,
        in_specs=(
            P(None, "dp", "head"),
            P(None, "dp", "head"),
            P(None, "dp", "head"),
            P(None, "dp", "head"),
            P(),
            P("dp", "head"),
            P("dp", "head"),
            P("head"),
            P("head"),
            P("dp", "head"),
            P("dp", "head"),
            P("head", "dp"),
        ),
        out_specs=(P("dp", "head"), P("dp", "head"), P("dp", "head")),
        check_vma=False,
    )
```

```python
import jax
import jax.numpy as jnp
from jax import lax
from jax.experimental import pallas as pl
from jax.experimental.pallas import tpu as pltpu
from jax.sharding import PartitionSpec as P

EPS = 1e-06
NX, NZ, NY, NC = 4, 8, 4, 2
AXES = ("dp", "head")
BF = jnp.bfloat16
F32 = jnp.float32
MIB = 56


def move(value, dx=0, dz=0, dy=0, dc=0):
    pairs = []
    for x in range(NX):
        for z in range(NZ):
            for y in range(NY):
                for c in range(NC):
                    src = (x * NZ + z) * 8 + y * NC + c
                    dst = (
                        ((x + dx) % NX * NZ + (z + dz) % NZ) * 8
                        + (y + dy) % NY * NC
                        + (c + dc) % NC
                    )
                    pairs.append((src, dst))
    return lax.ppermute(value, AXES, pairs)


def spread_columns(shard):
    pairs = []
    for x in range(NX):
        for z in range(NZ):
            for y in range(NY):
                for c in range(NC):
                    d, t = z // 4, z % 4
                    src = (x * NZ + z) * 8 + y * NC + c
                    pairs.append((src, (t * NZ + 4 * c + x) * 8 + y * NC + d))
    return lax.ppermute(shard, AXES, pairs)


def call(kernel, out_shape, n_scalar, n_array, flops, scratch=(), name=None, space=pltpu.VMEM):
    return pl.pallas_call(
        kernel,
        out_shape=out_shape,
        in_specs=[pl.BlockSpec(memory_space=pltpu.SMEM)] * n_scalar
        + [pl.BlockSpec(memory_space=space)] * n_array,
        out_specs=jax.tree.map(lambda _: pl.BlockSpec(memory_space=pltpu.VMEM), out_shape),
        scratch_shapes=scratch,
        compiler_params=pltpu.CompilerParams(vmem_limit_bytes=MIB * 1024 * 1024),
        cost_estimate=pl.CostEstimate(flops=flops, bytes_accessed=6_000_000, transcendentals=0),
        name=name,
    )


def dot_nt(a, b):
    return lax.dot_general(a, b, (((1,), (1,)), ((), ())), preferred_element_type=F32)


def dot_tn(a, b):
    return lax.dot_general(a, b, (((0,), (0,)), ((), ())), preferred_element_type=F32)


def part_kernel(where, core, *refs):
    pieces, outs, (wall, rows, sems) = refs[:8], refs[-7:-3], refs[-3:]
    count = (len(refs) - 15) // 2
    copies = []
    for k, ref in enumerate(pieces):
        at = pl.multiple_of(where[k] % 4 * 112, 16)
        spot = wall.at[where[k] // 4, pl.ds(at, 112)]
        copies.append(pltpu.make_async_copy(ref, spot, sems.at[k]))
    at = 0
    for k in range(count):
        size = refs[8 + k].shape[0]
        for side in range(2):
            spot = rows.at[side, pl.ds(at, size)]
            ref, sem = refs[8 + side * count + k], sems.at[8 + 2 * k + side]
            copies.append(pltpu.make_async_copy(ref, spot, sem))
        at += size
    for copy in copies:
        copy.start()
    for copy in copies[:8]:
        copy.wait()
    own, other = wall[core[0]], wall[1 - core[0]]
    at = 0
    for k in range(count):
        size = refs[8 + k].shape[0]
        copies[8 + 2 * k].wait()
        copies[9 + 2 * k].wait()
        prod = dot_nt(own, rows[0, at : at + size, :])
        prod = (prod + dot_nt(other, rows[1, at : at + size, :])).astype(BF)
        for k in range(4):
            outs[k][:, at : at + size] = prod[k * 112 : (k + 1) * 112, :]
        at += size


def send_kernel(xs, *refs):
    first, last, (lane_pos, out, moved) = refs[:4], refs[4:8], refs[8:]
    for r in range(4):
        parts, at = (first, r * 512) if r < 3 else (last, 0)
        total = parts[0][:, at : at + 512].astype(F32)
        for part in parts[1:]:
            total = total + part[:, at : at + 512].astype(F32)
        ids = lax.broadcasted_iota(jnp.int32, (1024, 512), 0)
        pick = jnp.where(ids == lane_pos[r : r + 1, :], 1.0, 0.0).astype(BF)
        moved[xs[r]] = dot_nt(total.astype(BF), pick).astype(BF)
    group = lax.broadcasted_iota(jnp.int32, (112, 128), 1) // 32
    for q in range(8):
        tiles = [moved[x, :, q * 128 : (q + 1) * 128] for x in range(4)]
        for j in range(4):
            here = tiles[(0 - j) % 4]
            for g in range(1, 4):
                here = jnp.where(group == g, tiles[(g - j) % 4], here)
            out[4 * q + j] = here


def stats_kernel(bundle, stats, held, sems):
    copies = []
    for k in range(8):
        rows = bundle.at[pl.ds(k * 912, 912)]
        copies.append(pltpu.make_async_copy(rows, held.at[k], sems.at[k]))
    for copy in copies:
        copy.start()
    for copy in copies:
        copy.wait()

    def out_sum(k, total):
        value = held[k, 448:896, :].astype(F32)
        return total + jnp.sum(value * value, axis=0, keepdims=True)

    total = lax.fori_loop(0, 8, out_sum, jnp.zeros((1, 512), F32))
    out_scale = lax.rsqrt(total / 3584.0 + EPS)

    def resid_sums(k, sums):
        gain = held[k, 896:912, :].astype(F32).T[:448, 0:1]
        gout = held[k, 448:896, :].astype(F32) * gain
        resid = held[k, 0:448, :].astype(F32) + gout * out_scale
        square = jnp.sum(resid * resid, axis=0, keepdims=True)
        return sums[0] + square, sums[1] + jnp.sum(resid * gout, axis=0, keepdims=True)

    zero = jnp.zeros((1, 512), F32)
    square, cross = lax.fori_loop(0, 8, resid_sums, (zero, zero))
    stats[...] = jnp.concatenate(
        [out_scale, lax.rsqrt(square / 3584.0 + EPS), cross, jnp.zeros((5, 512), F32)], axis=0
    )


def recv_kernel(arrived, row_pos, mid, out, gain_post, gain_final, stats, grad):
    ids = lax.broadcasted_iota(jnp.int32, (1024, 512), 0)
    pick = jnp.where(ids == row_pos[...], 1.0, 0.0).astype(BF)
    out_scale = stats[0:1, :]
    first = jnp.zeros((1, 512), F32)
    second = jnp.zeros((1, 512), F32)
    for x in range(4):
        side = jnp.concatenate([arrived[x * 8 + z] for z in range(8)], axis=1)
        rows = slice(x * 112, (x + 1) * 112)
        piece = jnp.dot(side, pick, preferred_element_type=F32)
        grad[rows, :] = piece.astype(BF)
        piece = piece * gain_final[rows, :]
        gout = out[rows, :].astype(F32) * gain_post[rows, :]
        resid = mid[rows, :].astype(F32) + gout * out_scale
        first = first + jnp.sum(piece * resid, axis=0, keepdims=True)
        second = second + jnp.sum(piece * gout, axis=0, keepdims=True)
    parts = []
    for value in (first, second):
        for _ in range(3):
            parts.append(value.astype(BF).astype(F32))
            value = value - parts[-1]
    parts.append(jnp.zeros((10, 512), F32))
    grad[448:464, :] = jnp.concatenate(parts, axis=0).astype(BF)


def row_factors(stats, grads):
    sums = grads[0, 448:464, :].astype(F32)
    for k in range(1, 8):
        sums = sums + grads[k, 448:464, :].astype(F32)
    first = sums[0:1, :] + sums[1:2, :] + sums[2:3, :]
    second = sums[3:4, :] + sums[4:5, :] + sums[5:6, :]
    out_scale, resid_scale, cross = stats[0:1, :], stats[1:2, :], stats[2:3, :]
    final_mean = resid_scale * first / 3584.0
    post_dot = resid_scale * (second - resid_scale * final_mean * cross)
    post_mean = out_scale * post_dot / 3584.0
    return out_scale, resid_scale, resid_scale * final_mean, out_scale * post_mean


def final_kernel(heads, *refs):
    grads, (weight, bundle, slope, active, stats, resid_grad, gate, up) = refs[:8], refs[8:16]
    grad_buf, weight_buf, held, scale_buf, stat_buf, value, sems = refs[16:]
    copies = [pltpu.make_async_copy(stats, stat_buf, sems.at[26])]
    for k in range(8):
        copies.append(pltpu.make_async_copy(grads[k], grad_buf.at[k], sems.at[k]))
    for k in range(8):
        at = pl.multiple_of(heads[k] * 448, 64)
        start = pl.multiple_of(heads[k] * 912, 16)
        rows = bundle.at[pl.ds(start, 912)]
        copies.append(pltpu.make_async_copy(rows, held.at[k], sems.at[8 + k]))
        rows = weight.at[pl.ds(at, 448)]
        copies.append(pltpu.make_async_copy(rows, weight_buf.at[k], sems.at[16 + k]))
    copies.append(pltpu.make_async_copy(slope, scale_buf.at[0], sems.at[24]))
    copies.append(pltpu.make_async_copy(active, scale_buf.at[1], sems.at[25]))
    for copy in copies:
        copy.start()
    for copy in copies[:9]:
        copy.wait()
    out_scale, resid_scale, pull, push = row_factors(stat_buf, grad_buf)
    value[...] = jnp.zeros((512, 896), F32)

    @pl.loop(0, 8)
    def _(k):
        pltpu.make_async_copy(bundle.at[pl.ds(0, 912)], held.at[k], sems.at[8 + k]).wait()
        pltpu.make_async_copy(weight.at[pl.ds(0, 448)], weight_buf.at[k], sems.at[16 + k]).wait()
        gains = held[k, 896:912, :].astype(F32).T
        gain_post, gain_final = gains[:448, 0:1], gains[:448, 1:2]
        out = held[k, 448:896, :].astype(F32)
        resid = held[k, 0:448, :].astype(F32) + out * gain_post * out_scale
        norm_grad = grad_buf[k, 0:448, :].astype(F32) * gain_final
        total = resid_scale * (norm_grad - resid * pull)

        @pl.when(k == 0)
        def _():
            resid_grad[...] = total.astype(BF)

        post = out_scale * (total * gain_post - out * push)
        value[...] += dot_tn(post.astype(BF), weight_buf[k])

    for copy in copies[25:]:
        copy.wait()
    gate[...] = (value[...] * scale_buf[0]).astype(BF)
    up[...] = (value[...] * scale_buf[1]).astype(BF)


def gelu_parts(gate_value):
    activated, pullback = jax.vjp(
        lambda pre_act: jax.nn.gelu(pre_act, approximate=True), gate_value
    )
    return (activated, pullback(jnp.ones_like(gate_value))[0])


def per_device(
    key_grads,
    value_grads,
    key_weight,
    value_weight,
    block_source,
    hidden_mid,
    mlp_out,
    post_gain,
    final_gain,
    gate_pre,
    up_pre,
    down_weight,
):
    dev = lax.axis_index("dp")
    head = lax.axis_index("head")
    x, z = dev // NZ, dev % NZ
    y, c = head // NC, head % NC

    weight = jnp.concatenate([key_weight[0], key_weight[1], value_weight[0], value_weight[1]], 1)
    weight, key_grads, value_grads = lax.optimization_barrier((weight, key_grads, value_grads))
    rows = jnp.concatenate([key_grads[0], key_grads[1], value_grads[0], value_grads[1]], 1)
    block_ids = jnp.arange(1024, dtype=jnp.int32)
    is_source = block_source[:, None] == block_ids[None, :]
    dest_block = jnp.sum(jnp.where(is_source, block_ids[:, None], 0), axis=0)
    dest_device = (dest_block // 32).reshape(32, 32)
    same_dest = dest_device[:, :, None] == dest_device[:, None, :]
    slot_ids = jnp.arange(32, dtype=jnp.int32)
    before = slot_ids[None, :] < slot_ids[:, None]
    rank = jnp.sum((same_dest & before[None]).astype(jnp.int32), axis=2)
    own_x = jnp.stack([x, (x + 3) % 4, (x + 1) % 4, (x + 2) % 4]).astype(jnp.int32)
    spread_ids = (own_x * NZ + z)[:, None, None] == slot_ids[None, :, None]
    dest_own = jnp.sum(jnp.where(spread_ids, dest_device[None], 0), axis=1)
    rank_own = jnp.sum(jnp.where(spread_ids, rank[None], 0), axis=1)
    lanes = (
        (dest_own // 4) * 128 + ((dest_own % 4 + own_x[:, None]) % 4) * 32 + rank_own * 16
    )
    lane_pos = (lanes[:, :, None] + jnp.arange(16, dtype=jnp.int32)).reshape(4, 512)
    source = lax.dynamic_slice_in_dim(block_source, dev * 32, 32)
    source_dev = source // 32
    source_rank = jnp.sum(
        jnp.where(block_ids[None, :] == source[:, None], rank.reshape(-1)[None, :], 0), axis=1
    )
    spot = (
        (source_dev % NZ) * 128 + ((dev % 4 + source_dev // NZ) % 4) * 32 + source_rank * 16
    )
    row_pos = (spot[:, None] + jnp.arange(16, dtype=jnp.int32)).reshape(1, 512)

    where = ((z - jnp.array([0, 1, 2, 3, 4, -1, -2, -3], jnp.int32)) % NZ).astype(jnp.int32)
    core = c.reshape(1).astype(jnp.int32)

    w0 = spread_columns(weight)
    s0 = move(rows, dc=1)
    gains = jnp.pad(jnp.stack([post_gain, final_gain]), ((0, 14), (0, 64)))
    bundle = jnp.concatenate([hidden_mid.T, mlp_out.T, gains], axis=0)
    bundle = lax.all_gather(bundle, "head", axis=0, tiled=True)
    w0, where = lax.optimization_barrier((w0, where))
    r1, r2 = move(rows, dx=1), move(rows, dx=-1)
    f1, g1 = move(w0, dz=1), move(w0, dz=-1)
    f2, g2 = move(f1, dz=1), move(g1, dz=-1)
    r1, r2, f2, g2, s0 = lax.optimization_barrier((r1, r2, f2, g2, s0))
    f3, g3 = move(f2, dz=1), move(g2, dz=-1)
    f4 = move(f3, dz=1)
    s1, s2 = move(r1, dc=1), move(r2, dc=1)
    r3 = move(r1, dx=1)

    gain_post = post_gain.astype(F32)[:, None]
    gain_final = final_gain.astype(F32)[:, None]
    active, slope = gelu_parts(gate_pre.astype(F32))
    slope = slope * up_pre.astype(F32)
    down_share, r1 = lax.optimization_barrier((down_weight.T, r1))
    down = lax.all_gather(down_share, "dp", axis=0, tiled=True)

    pieces = (w0, f1, f2, f3, f4, g1, g2, g3)

    place = (where // 4 * 4 + (where % 4 - y) % NY).astype(jnp.int32)

    def part(left, right):
        size = sum(ref.shape[0] for ref in left)
        parts = call(
            part_kernel,
            (jax.ShapeDtypeStruct((112, size), BF),) * 4,
            2,
            8 + 2 * len(left),
            2 * size * 448 * 2048,
            [
                pltpu.VMEM((2, 448, 1024), BF),
                pltpu.VMEM((2, size, 1024), BF),
                pltpu.SemaphoreType.DMA((8 + 2 * len(left),)),
            ],
            name="part",
            space=pl.ANY,
        )(place, core, *pieces, *left, *right)
        return parts

    def over_y(parts):
        return [parts[0]] + [move(parts[k], dy=k) for k in (2, 1, 3)]

    first = part((rows, r1, r2), (s0, s1, s2))
    first, r3 = lax.optimization_barrier((first, r3))
    last = part((r3,), (move(r3, dc=1),))
    groups = over_y(first) + over_y(last)
    groups[0], lane_pos, row_pos = lax.optimization_barrier((groups[0], lane_pos, row_pos))
    outgoing = call(
        send_kernel,
        jax.ShapeDtypeStruct((32, 112, 128), BF),
        1,
        len(groups) + 1,
        2 * 112 * 2048 * 1024,
        [pltpu.VMEM((4, 112, 1024), BF)],
        name="send",
    )(own_x, *groups, lane_pos)
    arrived = lax.all_to_all(outgoing, "dp", 0, 0, tiled=True)
    stats = call(
        stats_kernel,
        jax.ShapeDtypeStruct((8, 512), F32),
        0,
        1,
        3584 * 512 * 12,
        [pltpu.VMEM((8, 912, 512), BF), pltpu.SemaphoreType.DMA((8,))],
        name="stats",
        space=pl.ANY,
    )(bundle)
    arrived, stats, active, slope = lax.optimization_barrier((arrived, stats, active, slope))
    mid, out = hidden_mid.T, mlp_out.T
    grad = call(
        recv_kernel,
        jax.ShapeDtypeStruct((464, 512), BF),
        0,
        7,
        2 * 448 * 512 * 1024,
        name="recv",
    )(arrived, row_pos, mid, out, gain_post, gain_final, stats)
    p1, p2, p3 = move(grad, dy=1), move(grad, dy=-1), move(grad, dy=2)
    q0 = move(grad, dc=1)
    q1, q2, q3 = move(p1, dc=1), move(p2, dc=1), move(p3, dc=1)
    from_y = jnp.stack([y, y, y + 3, y + 3, y + 1, y + 1, y + 2, y + 2]) % 4
    from_c = (c + jnp.array([0, 1] * 4, jnp.int32)) % 2
    heads = (from_y * 2 + from_c).astype(jnp.int32)
    resid_grad, gate_grad, up_grad = call(
        final_kernel,
        (
            jax.ShapeDtypeStruct((448, 512), BF),
            jax.ShapeDtypeStruct((512, 896), BF),
            jax.ShapeDtypeStruct((512, 896), BF),
        ),
        1,
        13,
        2 * 512 * 896 * 3584,
        [
            pltpu.VMEM((8, 464, 512), BF),
            pltpu.VMEM((8, 448, 896), BF),
            pltpu.VMEM((8, 912, 512), BF),
            pltpu.VMEM((2, 512, 896), F32),
            pltpu.VMEM((8, 512), F32),
            pltpu.VMEM((512, 896), F32),
            pltpu.SemaphoreType.DMA((27,)),
        ],
        name="final",
        space=pl.ANY,
    )(heads, grad, q0, p1, q1, p2, q2, p3, q3, down, bundle, slope, active, stats)
    return (resid_grad.T, gate_grad, up_grad)


def solution(mesh):
    return jax.shard_map(
        per_device,
        mesh=mesh,
        in_specs=(
            P(None, "dp", "head"),
            P(None, "dp", "head"),
            P(None, "dp", "head"),
            P(None, "dp", "head"),
            P(),
            P("dp", "head"),
            P("dp", "head"),
            P("head"),
            P("head"),
            P("dp", "head"),
            P("dp", "head"),
            P("head", "dp"),
        ),
        out_specs=(P("dp", "head"), P("dp", "head"), P("dp", "head")),
        check_vma=False,
    )
```

```python
import jax
import jax.numpy as jnp
from jax import lax
from jax.experimental import pallas as pl
from jax.experimental.pallas import tpu as pltpu
from jax.sharding import PartitionSpec as P

EPS = 1e-06
NX, NZ, NY, NC = 4, 8, 4, 2
AXES = ("dp", "head")
BF = jnp.bfloat16
F32 = jnp.float32
MIB = 56


def move(value, dx=0, dz=0, dy=0, dc=0):
    pairs = []
    for x in range(NX):
        for z in range(NZ):
            for y in range(NY):
                for c in range(NC):
                    src = (x * NZ + z) * 8 + y * NC + c
                    dst = (
                        ((x + dx) % NX * NZ + (z + dz) % NZ) * 8
                        + (y + dy) % NY * NC
                        + (c + dc) % NC
                    )
                    pairs.append((src, dst))
    return lax.ppermute(value, AXES, pairs)


def spread_columns(shard):
    pairs = []
    for x in range(NX):
        for z in range(NZ):
            for y in range(NY):
                for c in range(NC):
                    d, t = z // 4, z % 4
                    src = (x * NZ + z) * 8 + y * NC + c
                    pairs.append((src, (t * NZ + 4 * c + x) * 8 + y * NC + d))
    return lax.ppermute(shard, AXES, pairs)


def call(kernel, out_shape, n_scalar, n_array, flops, scratch=(), name=None, space=pltpu.VMEM):
    return pl.pallas_call(
        kernel,
        out_shape=out_shape,
        in_specs=[pl.BlockSpec(memory_space=pltpu.SMEM)] * n_scalar
        + [pl.BlockSpec(memory_space=space)] * n_array,
        out_specs=jax.tree.map(lambda _: pl.BlockSpec(memory_space=pltpu.VMEM), out_shape),
        scratch_shapes=scratch,
        compiler_params=pltpu.CompilerParams(vmem_limit_bytes=MIB * 1024 * 1024),
        cost_estimate=pl.CostEstimate(flops=flops, bytes_accessed=6_000_000, transcendentals=0),
        name=name,
    )


def dot_nt(a, b):
    return lax.dot_general(a, b, (((1,), (1,)), ((), ())), preferred_element_type=F32)


def dot_tn(a, b):
    return lax.dot_general(a, b, (((0,), (0,)), ((), ())), preferred_element_type=F32)


def part_kernel(where, core, *refs):
    pieces, outs, (wall, rows, sems) = refs[:8], refs[-7:-3], refs[-3:]
    count = (len(refs) - 15) // 2
    copies = []
    for k, ref in enumerate(pieces):
        at = pl.multiple_of(where[k] % 4 * 112, 16)
        spot = wall.at[where[k] // 4, pl.ds(at, 112)]
        copies.append(pltpu.make_async_copy(ref, spot, sems.at[k]))
    at = 0
    for k in range(count):
        size = refs[8 + k].shape[0]
        for side in range(2):
            spot = rows.at[side, pl.ds(at, size)]
            ref, sem = refs[8 + side * count + k], sems.at[8 + 2 * k + side]
            copies.append(pltpu.make_async_copy(ref, spot, sem))
        at += size
    for copy in copies:
        copy.start()
    for copy in copies[:8]:
        copy.wait()
    own, other = wall[core[0]], wall[1 - core[0]]
    at = 0
    for k in range(count):
        size = refs[8 + k].shape[0]
        copies[8 + 2 * k].wait()
        copies[9 + 2 * k].wait()
        prod = dot_nt(own, rows[0, at : at + size, :])
        prod = (prod + dot_nt(other, rows[1, at : at + size, :])).astype(BF)
        for k in range(4):
            outs[k][:, at : at + size] = prod[k * 112 : (k + 1) * 112, :]
        at += size


def send_kernel(xs, *refs):
    first, last, (lane_pos, out, moved) = refs[:4], refs[4:8], refs[8:]
    for r in range(4):
        parts, at = (first, r * 512) if r < 3 else (last, 0)
        total = parts[0][:, at : at + 512].astype(F32)
        for part in parts[1:]:
            total = total + part[:, at : at + 512].astype(F32)
        ids = lax.broadcasted_iota(jnp.int32, (1024, 512), 0)
        pick = jnp.where(ids == lane_pos[r : r + 1, :], 1.0, 0.0).astype(BF)
        moved[xs[r]] = dot_nt(total.astype(BF), pick).astype(BF)
    group = lax.broadcasted_iota(jnp.int32, (112, 128), 1) // 32
    for q in range(8):
        tiles = [moved[x, :, q * 128 : (q + 1) * 128] for x in range(4)]
        for j in range(4):
            here = tiles[(0 - j) % 4]
            for g in range(1, 4):
                here = jnp.where(group == g, tiles[(g - j) % 4], here)
            out[4 * q + j] = here


def stats_kernel(bundle, stats, held, sems):
    copies = []
    for k in range(8):
        rows = bundle.at[pl.ds(k * 912, 912)]
        copies.append(pltpu.make_async_copy(rows, held.at[k], sems.at[k]))
    for copy in copies:
        copy.start()
    for copy in copies:
        copy.wait()

    def out_sum(k, total):
        value = held[k, 448:896, :].astype(F32)
        return total + jnp.sum(value * value, axis=0, keepdims=True)

    total = lax.fori_loop(0, 8, out_sum, jnp.zeros((1, 512), F32))
    out_scale = lax.rsqrt(total / 3584.0 + EPS)

    def resid_sums(k, sums):
        gain = held[k, 896:912, :].astype(F32).T[:448, 0:1]
        gout = held[k, 448:896, :].astype(F32) * gain
        resid = held[k, 0:448, :].astype(F32) + gout * out_scale
        square = jnp.sum(resid * resid, axis=0, keepdims=True)
        return sums[0] + square, sums[1] + jnp.sum(resid * gout, axis=0, keepdims=True)

    zero = jnp.zeros((1, 512), F32)
    square, cross = lax.fori_loop(0, 8, resid_sums, (zero, zero))
    stats[...] = jnp.concatenate(
        [out_scale, lax.rsqrt(square / 3584.0 + EPS), cross, jnp.zeros((5, 512), F32)], axis=0
    )


def recv_kernel(arrived, row_pos, mid, out, gain_post, gain_final, stats, grad):
    ids = lax.broadcasted_iota(jnp.int32, (1024, 512), 0)
    pick = jnp.where(ids == row_pos[...], 1.0, 0.0).astype(BF)
    out_scale = stats[0:1, :]
    first = jnp.zeros((1, 512), F32)
    second = jnp.zeros((1, 512), F32)
    for x in range(4):
        side = jnp.concatenate([arrived[x * 8 + z] for z in range(8)], axis=1)
        rows = slice(x * 112, (x + 1) * 112)
        piece = jnp.dot(side, pick, preferred_element_type=F32)
        grad[rows, :] = piece.astype(BF)
        piece = piece * gain_final[rows, :]
        gout = out[rows, :].astype(F32) * gain_post[rows, :]
        resid = mid[rows, :].astype(F32) + gout * out_scale
        first = first + jnp.sum(piece * resid, axis=0, keepdims=True)
        second = second + jnp.sum(piece * gout, axis=0, keepdims=True)
    parts = []
    for value in (first, second):
        for _ in range(3):
            parts.append(value.astype(BF).astype(F32))
            value = value - parts[-1]
    parts.append(jnp.zeros((10, 512), F32))
    grad[448:464, :] = jnp.concatenate(parts, axis=0).astype(BF)


def row_factors(stats, grads):
    sums = grads[0, 448:464, :].astype(F32)
    for k in range(1, 8):
        sums = sums + grads[k, 448:464, :].astype(F32)
    first = sums[0:1, :] + sums[1:2, :] + sums[2:3, :]
    second = sums[3:4, :] + sums[4:5, :] + sums[5:6, :]
    out_scale, resid_scale, cross = stats[0:1, :], stats[1:2, :], stats[2:3, :]
    final_mean = resid_scale * first / 3584.0
    post_dot = resid_scale * (second - resid_scale * final_mean * cross)
    post_mean = out_scale * post_dot / 3584.0
    return out_scale, resid_scale, resid_scale * final_mean, out_scale * post_mean


def final_kernel(heads, *refs):
    grads, (weight, bundle, slope, active, stats, resid_grad, gate, up) = refs[:8], refs[8:16]
    grad_buf, weight_buf, held, scale_buf, stat_buf, value, even, odd, sems = refs[16:]
    copies = [pltpu.make_async_copy(stats, stat_buf, sems.at[26])]
    for k in range(8):
        copies.append(pltpu.make_async_copy(grads[k], grad_buf.at[k], sems.at[k]))
    for k in range(8):
        at = pl.multiple_of(heads[k] * 448, 64)
        start = pl.multiple_of(heads[k] * 912, 16)
        rows = bundle.at[pl.ds(start, 912)]
        copies.append(pltpu.make_async_copy(rows, held.at[k], sems.at[8 + k]))
        rows = weight.at[pl.ds(at, 448)]
        copies.append(pltpu.make_async_copy(rows, weight_buf.at[k], sems.at[16 + k]))
    copies.append(pltpu.make_async_copy(slope, scale_buf.at[0], sems.at[24]))
    copies.append(pltpu.make_async_copy(active, scale_buf.at[1], sems.at[25]))
    for copy in copies:
        copy.start()
    for copy in copies[:9]:
        copy.wait()
    out_scale, resid_scale, pull, push = row_factors(stat_buf, grad_buf)

    def arrive(k):
        pltpu.make_async_copy(bundle.at[pl.ds(0, 912)], held.at[k], sems.at[8 + k]).wait()
        pltpu.make_async_copy(weight.at[pl.ds(0, 448)], weight_buf.at[k], sems.at[16 + k]).wait()

    def totals(k):
        gains = held[k, 896:912, :].astype(F32).T
        gain_post, gain_final = gains[:448, 0:1], gains[:448, 1:2]
        out = held[k, 448:896, :].astype(F32)
        resid = held[k, 0:448, :].astype(F32) + out * gain_post * out_scale
        norm_grad = grad_buf[k, 0:448, :].astype(F32) * gain_final
        total = resid_scale * (norm_grad - resid * pull)
        return total, (out_scale * (total * gain_post - out * push)).astype(BF)

    arrive(0)
    total, post = totals(0)
    resid_grad[...] = total.astype(BF)
    even[...] = post
    value[...] = jnp.zeros((512, 896), F32)

    @pl.loop(0, 4)
    def _(pair):
        arrive(2 * pair + 1)
        odd[...] = totals(2 * pair + 1)[1]
        value[...] += dot_tn(even[...], weight_buf[2 * pair])

        @pl.when(pair < 3)
        def _():
            arrive(2 * pair + 2)

        even[...] = totals(jnp.minimum(2 * pair + 2, 7))[1]
        value[...] += dot_tn(odd[...], weight_buf[2 * pair + 1])

    for copy in copies[25:]:
        copy.wait()
    gate[...] = (value[...] * scale_buf[0]).astype(BF)
    up[...] = (value[...] * scale_buf[1]).astype(BF)


def gelu_parts(gate_value):
    activated, pullback = jax.vjp(
        lambda pre_act: jax.nn.gelu(pre_act, approximate=True), gate_value
    )
    return (activated, pullback(jnp.ones_like(gate_value))[0])


def per_device(
    key_grads,
    value_grads,
    key_weight,
    value_weight,
    block_source,
    hidden_mid,
    mlp_out,
    post_gain,
    final_gain,
    gate_pre,
    up_pre,
    down_weight,
):
    dev = lax.axis_index("dp")
    head = lax.axis_index("head")
    x, z = dev // NZ, dev % NZ
    y, c = head // NC, head % NC

    weight = jnp.concatenate([key_weight[0], key_weight[1], value_weight[0], value_weight[1]], 1)
    weight, key_grads, value_grads = lax.optimization_barrier((weight, key_grads, value_grads))
    rows = jnp.concatenate([key_grads[0], key_grads[1], value_grads[0], value_grads[1]], 1)
    block_ids = jnp.arange(1024, dtype=jnp.int32)
    is_source = block_source[:, None] == block_ids[None, :]
    dest_block = jnp.sum(jnp.where(is_source, block_ids[:, None], 0), axis=0)
    dest_device = (dest_block // 32).reshape(32, 32)
    same_dest = dest_device[:, :, None] == dest_device[:, None, :]
    slot_ids = jnp.arange(32, dtype=jnp.int32)
    before = slot_ids[None, :] < slot_ids[:, None]
    rank = jnp.sum((same_dest & before[None]).astype(jnp.int32), axis=2)
    own_x = jnp.stack([x, (x + 3) % 4, (x + 1) % 4, (x + 2) % 4]).astype(jnp.int32)
    spread_ids = (own_x * NZ + z)[:, None, None] == slot_ids[None, :, None]
    dest_own = jnp.sum(jnp.where(spread_ids, dest_device[None], 0), axis=1)
    rank_own = jnp.sum(jnp.where(spread_ids, rank[None], 0), axis=1)
    lanes = (
        (dest_own // 4) * 128 + ((dest_own % 4 + own_x[:, None]) % 4) * 32 + rank_own * 16
    )
    lane_pos = (lanes[:, :, None] + jnp.arange(16, dtype=jnp.int32)).reshape(4, 512)
    source = lax.dynamic_slice_in_dim(block_source, dev * 32, 32)
    source_dev = source // 32
    source_rank = jnp.sum(
        jnp.where(block_ids[None, :] == source[:, None], rank.reshape(-1)[None, :], 0), axis=1
    )
    spot = (
        (source_dev % NZ) * 128 + ((dev % 4 + source_dev // NZ) % 4) * 32 + source_rank * 16
    )
    row_pos = (spot[:, None] + jnp.arange(16, dtype=jnp.int32)).reshape(1, 512)

    where = ((z - jnp.array([0, 1, 2, 3, 4, -1, -2, -3], jnp.int32)) % NZ).astype(jnp.int32)
    core = c.reshape(1).astype(jnp.int32)

    w0 = spread_columns(weight)
    s0 = move(rows, dc=1)
    gains = jnp.pad(jnp.stack([post_gain, final_gain]), ((0, 14), (0, 64)))
    bundle = jnp.concatenate([hidden_mid.T, mlp_out.T, gains], axis=0)
    bundle = lax.all_gather(bundle, "head", axis=0, tiled=True)
    w0, where = lax.optimization_barrier((w0, where))
    r1, r2 = move(rows, dx=1), move(rows, dx=-1)
    f1, g1 = move(w0, dz=1), move(w0, dz=-1)
    f2, g2 = move(f1, dz=1), move(g1, dz=-1)
    r1, r2, f2, g2, s0 = lax.optimization_barrier((r1, r2, f2, g2, s0))
    f3, g3 = move(f2, dz=1), move(g2, dz=-1)
    f4 = move(f3, dz=1)
    s1, s2 = move(r1, dc=1), move(r2, dc=1)
    r3 = move(r1, dx=1)

    gain_post = post_gain.astype(F32)[:, None]
    gain_final = final_gain.astype(F32)[:, None]
    active, slope = gelu_parts(gate_pre.astype(F32))
    slope = slope * up_pre.astype(F32)
    down_share, r1 = lax.optimization_barrier((down_weight.T, r1))
    down = lax.all_gather(down_share, "dp", axis=0, tiled=True)

    pieces = (w0, f1, f2, f3, f4, g1, g2, g3)

    place = (where // 4 * 4 + (where % 4 - y) % NY).astype(jnp.int32)

    def part(left, right):
        size = sum(ref.shape[0] for ref in left)
        parts = call(
            part_kernel,
            (jax.ShapeDtypeStruct((112, size), BF),) * 4,
            2,
            8 + 2 * len(left),
            2 * size * 448 * 2048,
            [
                pltpu.VMEM((2, 448, 1024), BF),
                pltpu.VMEM((2, size, 1024), BF),
                pltpu.SemaphoreType.DMA((8 + 2 * len(left),)),
            ],
            name="part",
            space=pl.ANY,
        )(place, core, *pieces, *left, *right)
        return parts

    def over_y(parts):
        return [parts[0]] + [move(parts[k], dy=k) for k in (2, 1, 3)]

    first = part((rows, r1, r2), (s0, s1, s2))
    first, r3 = lax.optimization_barrier((first, r3))
    last = part((r3,), (move(r3, dc=1),))
    groups = over_y(first) + over_y(last)
    groups[0], lane_pos, row_pos = lax.optimization_barrier((groups[0], lane_pos, row_pos))
    outgoing = call(
        send_kernel,
        jax.ShapeDtypeStruct((32, 112, 128), BF),
        1,
        len(groups) + 1,
        2 * 112 * 2048 * 1024,
        [pltpu.VMEM((4, 112, 1024), BF)],
        name="send",
    )(own_x, *groups, lane_pos)
    arrived = lax.all_to_all(outgoing, "dp", 0, 0, tiled=True)
    stats = call(
        stats_kernel,
        jax.ShapeDtypeStruct((8, 512), F32),
        0,
        1,
        3584 * 512 * 12,
        [pltpu.VMEM((8, 912, 512), BF), pltpu.SemaphoreType.DMA((8,))],
        name="stats",
        space=pl.ANY,
    )(bundle)
    arrived, stats, active, slope = lax.optimization_barrier((arrived, stats, active, slope))
    mid, out = hidden_mid.T, mlp_out.T
    grad = call(
        recv_kernel,
        jax.ShapeDtypeStruct((464, 512), BF),
        0,
        7,
        2 * 448 * 512 * 1024,
        name="recv",
    )(arrived, row_pos, mid, out, gain_post, gain_final, stats)
    p1, p2, p3 = move(grad, dy=1), move(grad, dy=-1), move(grad, dy=2)
    q0 = move(grad, dc=1)
    q1, q2, q3 = move(p1, dc=1), move(p2, dc=1), move(p3, dc=1)
    from_y = jnp.stack([y, y, y + 3, y + 3, y + 1, y + 1, y + 2, y + 2]) % 4
    from_c = (c + jnp.array([0, 1] * 4, jnp.int32)) % 2
    heads = (from_y * 2 + from_c).astype(jnp.int32)
    resid_grad, gate_grad, up_grad = call(
        final_kernel,
        (
            jax.ShapeDtypeStruct((448, 512), BF),
            jax.ShapeDtypeStruct((512, 896), BF),
            jax.ShapeDtypeStruct((512, 896), BF),
        ),
        1,
        13,
        2 * 512 * 896 * 3584,
        [
            pltpu.VMEM((8, 464, 512), BF),
            pltpu.VMEM((8, 448, 896), BF),
            pltpu.VMEM((8, 912, 512), BF),
            pltpu.VMEM((2, 512, 896), F32),
            pltpu.VMEM((8, 512), F32),
            pltpu.VMEM((512, 896), F32),
            pltpu.VMEM((448, 512), BF),
            pltpu.VMEM((448, 512), BF),
            pltpu.SemaphoreType.DMA((27,)),
        ],
        name="final",
        space=pl.ANY,
    )(heads, grad, q0, p1, q1, p2, q2, p3, q3, down, bundle, slope, active, stats)
    return (resid_grad.T, gate_grad, up_grad)


def solution(mesh):
    return jax.shard_map(
        per_device,
        mesh=mesh,
        in_specs=(
            P(None, "dp", "head"),
            P(None, "dp", "head"),
            P(None, "dp", "head"),
            P(None, "dp", "head"),
            P(),
            P("dp", "head"),
            P("dp", "head"),
            P("head"),
            P("head"),
            P("dp", "head"),
            P("dp", "head"),
            P("head", "dp"),
        ),
        out_specs=(P("dp", "head"), P("dp", "head"), P("dp", "head")),
        check_vma=False,
    )
```

```python
import jax
import jax.numpy as jnp
from jax import lax
from jax.experimental import pallas as pl
from jax.experimental.pallas import tpu as pltpu
from jax.sharding import PartitionSpec as P

EPS = 1e-06
NX, NZ, NY, NC = 4, 8, 4, 2
AXES = ("dp", "head")
BF = jnp.bfloat16
F32 = jnp.float32
MIB = 56


def move(value, dx=0, dz=0, dy=0, dc=0):
    pairs = []
    for x in range(NX):
        for z in range(NZ):
            for y in range(NY):
                for c in range(NC):
                    src = (x * NZ + z) * 8 + y * NC + c
                    dst = (
                        ((x + dx) % NX * NZ + (z + dz) % NZ) * 8
                        + (y + dy) % NY * NC
                        + (c + dc) % NC
                    )
                    pairs.append((src, dst))
    return lax.ppermute(value, AXES, pairs)


def spread_columns(shard):
    pairs = []
    for x in range(NX):
        for z in range(NZ):
            for y in range(NY):
                for c in range(NC):
                    d, t = z // 4, z % 4
                    src = (x * NZ + z) * 8 + y * NC + c
                    pairs.append((src, (t * NZ + 4 * c + x) * 8 + y * NC + d))
    return lax.ppermute(shard, AXES, pairs)


def call(kernel, out_shape, n_scalar, n_array, flops, scratch=(), name=None, space=pltpu.VMEM):
    return pl.pallas_call(
        kernel,
        out_shape=out_shape,
        in_specs=[pl.BlockSpec(memory_space=pltpu.SMEM)] * n_scalar
        + [pl.BlockSpec(memory_space=space)] * n_array,
        out_specs=jax.tree.map(lambda _: pl.BlockSpec(memory_space=pltpu.VMEM), out_shape),
        scratch_shapes=scratch,
        compiler_params=pltpu.CompilerParams(vmem_limit_bytes=MIB * 1024 * 1024),
        cost_estimate=pl.CostEstimate(flops=flops, bytes_accessed=6_000_000, transcendentals=0),
        name=name,
    )


def dot_nt(a, b):
    return lax.dot_general(a, b, (((1,), (1,)), ((), ())), preferred_element_type=F32)


def dot_tn(a, b):
    return lax.dot_general(a, b, (((0,), (0,)), ((), ())), preferred_element_type=F32)


def part_kernel(where, core, *refs):
    pieces, outs, (wall, rows, sems) = refs[:8], refs[-7:-3], refs[-3:]
    count = (len(refs) - 15) // 2
    copies = []
    for k, ref in enumerate(pieces):
        at = pl.multiple_of(where[k] % 4 * 112, 16)
        spot = wall.at[where[k] // 4, pl.ds(at, 112)]
        copies.append(pltpu.make_async_copy(ref, spot, sems.at[k]))
    at = 0
    for k in range(count):
        size = refs[8 + k].shape[0]
        for side in range(2):
            spot = rows.at[side, pl.ds(at, size)]
            ref, sem = refs[8 + side * count + k], sems.at[8 + 2 * k + side]
            copies.append(pltpu.make_async_copy(ref, spot, sem))
        at += size
    for copy in copies:
        copy.start()
    for copy in copies[:8]:
        copy.wait()
    own, other = wall[core[0]], wall[1 - core[0]]
    at = 0
    for k in range(count):
        size = refs[8 + k].shape[0]
        copies[8 + 2 * k].wait()
        copies[9 + 2 * k].wait()
        prod = dot_nt(own, rows[0, at : at + size, :])
        prod = (prod + dot_nt(other, rows[1, at : at + size, :])).astype(BF)
        for k in range(4):
            outs[k][:, at : at + size] = prod[k * 112 : (k + 1) * 112, :]
        at += size


def send_kernel(xs, *refs):
    first, last, (lane_pos, out, moved) = refs[:4], refs[4:8], refs[8:]
    for r in range(4):
        parts, at = (first, r * 512) if r < 3 else (last, 0)
        total = parts[0][:, at : at + 512].astype(F32)
        for part in parts[1:]:
            total = total + part[:, at : at + 512].astype(F32)
        ids = lax.broadcasted_iota(jnp.int32, (1024, 512), 0)
        pick = jnp.where(ids == lane_pos[r : r + 1, :], 1.0, 0.0).astype(BF)
        moved[xs[r]] = dot_nt(total.astype(BF), pick).astype(BF)
    group = lax.broadcasted_iota(jnp.int32, (112, 128), 1) // 32
    for q in range(8):
        tiles = [moved[x, :, q * 128 : (q + 1) * 128] for x in range(4)]
        for j in range(4):
            here = tiles[(0 - j) % 4]
            for g in range(1, 4):
                here = jnp.where(group == g, tiles[(g - j) % 4], here)
            out[4 * q + j] = here


def stats_kernel(bundle, stats, held, sems):
    copies = []
    for k in range(8):
        rows = bundle.at[pl.ds(k * 912, 912)]
        copies.append(pltpu.make_async_copy(rows, held.at[k], sems.at[k]))
    for copy in copies:
        copy.start()
    for copy in copies:
        copy.wait()

    def out_sum(k, total):
        value = held[k, 448:896, :].astype(F32)
        return total + jnp.sum(value * value, axis=0, keepdims=True)

    total = lax.fori_loop(0, 8, out_sum, jnp.zeros((1, 512), F32))
    out_scale = lax.rsqrt(total / 3584.0 + EPS)

    def resid_sums(k, sums):
        gain = held[k, 896:912, :].astype(F32).T[:448, 0:1]
        gout = held[k, 448:896, :].astype(F32) * gain
        resid = held[k, 0:448, :].astype(F32) + gout * out_scale
        square = jnp.sum(resid * resid, axis=0, keepdims=True)
        return sums[0] + square, sums[1] + jnp.sum(resid * gout, axis=0, keepdims=True)

    zero = jnp.zeros((1, 512), F32)
    square, cross = lax.fori_loop(0, 8, resid_sums, (zero, zero))
    stats[...] = jnp.concatenate(
        [out_scale, lax.rsqrt(square / 3584.0 + EPS), cross, jnp.zeros((5, 512), F32)], axis=0
    )


def recv_kernel(arrived, row_pos, mid, out, gain_post, gain_final, stats, grad):
    ids = lax.broadcasted_iota(jnp.int32, (1024, 512), 0)
    pick = jnp.where(ids == row_pos[...], 1.0, 0.0).astype(BF)
    out_scale = stats[0:1, :]
    first = jnp.zeros((1, 512), F32)
    second = jnp.zeros((1, 512), F32)
    for x in range(4):
        side = jnp.concatenate([arrived[x * 8 + z] for z in range(8)], axis=1)
        rows = slice(x * 112, (x + 1) * 112)
        piece = jnp.dot(side, pick, preferred_element_type=F32)
        grad[rows, :] = piece.astype(BF)
        piece = piece * gain_final[rows, :]
        gout = out[rows, :].astype(F32) * gain_post[rows, :]
        resid = mid[rows, :].astype(F32) + gout * out_scale
        first = first + jnp.sum(piece * resid, axis=0, keepdims=True)
        second = second + jnp.sum(piece * gout, axis=0, keepdims=True)
    parts = []
    for value in (first, second):
        for _ in range(3):
            parts.append(value.astype(BF).astype(F32))
            value = value - parts[-1]
    parts.append(jnp.zeros((10, 512), F32))
    grad[448:464, :] = jnp.concatenate(parts, axis=0).astype(BF)


def row_factors(stats, grads):
    sums = grads[0, 448:464, :].astype(F32)
    for k in range(1, 8):
        sums = sums + grads[k, 448:464, :].astype(F32)
    first = sums[0:1, :] + sums[1:2, :] + sums[2:3, :]
    second = sums[3:4, :] + sums[4:5, :] + sums[5:6, :]
    out_scale, resid_scale, cross = stats[0:1, :], stats[1:2, :], stats[2:3, :]
    final_mean = resid_scale * first / 3584.0
    post_dot = resid_scale * (second - resid_scale * final_mean * cross)
    post_mean = out_scale * post_dot / 3584.0
    return out_scale, resid_scale, resid_scale * final_mean, out_scale * post_mean


def final_kernel(heads, *refs):
    grads, (weight, bundle, slope, active, stats, resid_grad, gate, up) = refs[:8], refs[8:16]
    grad_buf, weight_buf, held, scale_buf, stat_buf, value, even, odd, sems = refs[16:]
    copies = [pltpu.make_async_copy(stats, stat_buf, sems.at[26])]
    for k in range(8):
        copies.append(pltpu.make_async_copy(grads[k], grad_buf.at[k], sems.at[k]))
    for k in range(8):
        at = pl.multiple_of(heads[k] * 448, 64)
        start = pl.multiple_of(heads[k] * 912, 16)
        rows = bundle.at[pl.ds(start, 912)]
        copies.append(pltpu.make_async_copy(rows, held.at[k], sems.at[8 + k]))
        rows = weight.at[pl.ds(at, 448)]
        copies.append(pltpu.make_async_copy(rows, weight_buf.at[k], sems.at[16 + k]))
    copies.append(pltpu.make_async_copy(slope, scale_buf.at[0], sems.at[24]))
    copies.append(pltpu.make_async_copy(active, scale_buf.at[1], sems.at[25]))
    for copy in copies:
        copy.start()
    value[...] = jnp.zeros((512, 896), F32)
    for copy in copies[:9]:
        copy.wait()
    out_scale, resid_scale, pull, push = row_factors(stat_buf, grad_buf)

    def arrive(k):
        pltpu.make_async_copy(bundle.at[pl.ds(0, 912)], held.at[k], sems.at[8 + k]).wait()
        pltpu.make_async_copy(weight.at[pl.ds(0, 448)], weight_buf.at[k], sems.at[16 + k]).wait()

    def totals(k):
        gains = held[k, 896:912, :].astype(F32).T
        gain_post, gain_final = gains[:448, 0:1], gains[:448, 1:2]
        out = held[k, 448:896, :].astype(F32)
        resid = held[k, 0:448, :].astype(F32) + out * gain_post * out_scale
        norm_grad = grad_buf[k, 0:448, :].astype(F32) * gain_final
        total = resid_scale * (norm_grad - resid * pull)
        return total, (out_scale * (total * gain_post - out * push)).astype(BF)

    arrive(0)
    total, post = totals(0)
    resid_grad[...] = total.astype(BF)
    even[...] = post

    @pl.loop(0, 4)
    def _(pair):
        arrive(2 * pair + 1)
        odd[...] = totals(2 * pair + 1)[1]
        value[...] += dot_tn(even[...], weight_buf[2 * pair])

        @pl.when(pair < 3)
        def _():
            arrive(2 * pair + 2)

        even[...] = totals(jnp.minimum(2 * pair + 2, 7))[1]
        value[...] += dot_tn(odd[...], weight_buf[2 * pair + 1])

    for copy in copies[25:]:
        copy.wait()
    gate[...] = (value[...] * scale_buf[0]).astype(BF)
    up[...] = (value[...] * scale_buf[1]).astype(BF)


def gelu_parts(gate_value):
    activated, pullback = jax.vjp(
        lambda pre_act: jax.nn.gelu(pre_act, approximate=True), gate_value
    )
    return (activated, pullback(jnp.ones_like(gate_value))[0])


def per_device(
    key_grads,
    value_grads,
    key_weight,
    value_weight,
    block_source,
    hidden_mid,
    mlp_out,
    post_gain,
    final_gain,
    gate_pre,
    up_pre,
    down_weight,
):
    dev = lax.axis_index("dp")
    head = lax.axis_index("head")
    x, z = dev // NZ, dev % NZ
    y, c = head // NC, head % NC

    weight = jnp.concatenate([key_weight[0], key_weight[1], value_weight[0], value_weight[1]], 1)
    weight, key_grads, value_grads = lax.optimization_barrier((weight, key_grads, value_grads))
    rows = jnp.concatenate([key_grads[0], key_grads[1], value_grads[0], value_grads[1]], 1)
    block_ids = jnp.arange(1024, dtype=jnp.int32)
    is_source = block_source[:, None] == block_ids[None, :]
    dest_block = jnp.sum(jnp.where(is_source, block_ids[:, None], 0), axis=0)
    dest_device = (dest_block // 32).reshape(32, 32)
    same_dest = dest_device[:, :, None] == dest_device[:, None, :]
    slot_ids = jnp.arange(32, dtype=jnp.int32)
    before = slot_ids[None, :] < slot_ids[:, None]
    rank = jnp.sum((same_dest & before[None]).astype(jnp.int32), axis=2)
    own_x = jnp.stack([x, (x + 3) % 4, (x + 1) % 4, (x + 2) % 4]).astype(jnp.int32)
    spread_ids = (own_x * NZ + z)[:, None, None] == slot_ids[None, :, None]
    dest_own = jnp.sum(jnp.where(spread_ids, dest_device[None], 0), axis=1)
    rank_own = jnp.sum(jnp.where(spread_ids, rank[None], 0), axis=1)
    lanes = (
        (dest_own // 4) * 128 + ((dest_own % 4 + own_x[:, None]) % 4) * 32 + rank_own * 16
    )
    lane_pos = (lanes[:, :, None] + jnp.arange(16, dtype=jnp.int32)).reshape(4, 512)
    source = lax.dynamic_slice_in_dim(block_source, dev * 32, 32)
    source_dev = source // 32
    source_rank = jnp.sum(
        jnp.where(block_ids[None, :] == source[:, None], rank.reshape(-1)[None, :], 0), axis=1
    )
    spot = (
        (source_dev % NZ) * 128 + ((dev % 4 + source_dev // NZ) % 4) * 32 + source_rank * 16
    )
    row_pos = (spot[:, None] + jnp.arange(16, dtype=jnp.int32)).reshape(1, 512)

    where = ((z - jnp.array([0, 1, 2, 3, 4, -1, -2, -3], jnp.int32)) % NZ).astype(jnp.int32)
    core = c.reshape(1).astype(jnp.int32)

    w0 = spread_columns(weight)
    s0 = move(rows, dc=1)
    gains = jnp.pad(jnp.stack([post_gain, final_gain]), ((0, 14), (0, 64)))
    bundle = jnp.concatenate([hidden_mid.T, mlp_out.T, gains], axis=0)
    bundle = lax.all_gather(bundle, "head", axis=0, tiled=True)
    w0, where = lax.optimization_barrier((w0, where))
    r1, r2 = move(rows, dx=1), move(rows, dx=-1)
    f1, g1 = move(w0, dz=1), move(w0, dz=-1)
    f2, g2 = move(f1, dz=1), move(g1, dz=-1)
    r1, r2, f2, g2, s0 = lax.optimization_barrier((r1, r2, f2, g2, s0))
    f3, g3 = move(f2, dz=1), move(g2, dz=-1)
    f4 = move(f3, dz=1)
    s1, s2 = move(r1, dc=1), move(r2, dc=1)
    r3 = move(r1, dx=1)

    gain_post = post_gain.astype(F32)[:, None]
    gain_final = final_gain.astype(F32)[:, None]
    active, slope = gelu_parts(gate_pre.astype(F32))
    slope = slope * up_pre.astype(F32)
    down_share, r1 = lax.optimization_barrier((down_weight.T, r1))
    down = lax.all_gather(down_share, "dp", axis=0, tiled=True)

    pieces = (w0, f1, f2, f3, f4, g1, g2, g3)

    place = (where // 4 * 4 + (where % 4 - y) % NY).astype(jnp.int32)

    def part(left, right):
        size = sum(ref.shape[0] for ref in left)
        parts = call(
            part_kernel,
            (jax.ShapeDtypeStruct((112, size), BF),) * 4,
            2,
            8 + 2 * len(left),
            2 * size * 448 * 2048,
            [
                pltpu.VMEM((2, 448, 1024), BF),
                pltpu.VMEM((2, size, 1024), BF),
                pltpu.SemaphoreType.DMA((8 + 2 * len(left),)),
            ],
            name="part",
            space=pl.ANY,
        )(place, core, *pieces, *left, *right)
        return parts

    def over_y(parts):
        return [parts[0]] + [move(parts[k], dy=k) for k in (2, 1, 3)]

    first = part((rows, r1, r2), (s0, s1, s2))
    first, r3 = lax.optimization_barrier((first, r3))
    last = part((r3,), (move(r3, dc=1),))
    groups = over_y(first) + over_y(last)
    groups[0], lane_pos, row_pos = lax.optimization_barrier((groups[0], lane_pos, row_pos))
    outgoing = call(
        send_kernel,
        jax.ShapeDtypeStruct((32, 112, 128), BF),
        1,
        len(groups) + 1,
        2 * 112 * 2048 * 1024,
        [pltpu.VMEM((4, 112, 1024), BF)],
        name="send",
    )(own_x, *groups, lane_pos)
    arrived = lax.all_to_all(outgoing, "dp", 0, 0, tiled=True)
    stats = call(
        stats_kernel,
        jax.ShapeDtypeStruct((8, 512), F32),
        0,
        1,
        3584 * 512 * 12,
        [pltpu.VMEM((8, 912, 512), BF), pltpu.SemaphoreType.DMA((8,))],
        name="stats",
        space=pl.ANY,
    )(bundle)
    arrived, stats, active, slope = lax.optimization_barrier((arrived, stats, active, slope))
    mid, out = hidden_mid.T, mlp_out.T
    grad = call(
        recv_kernel,
        jax.ShapeDtypeStruct((464, 512), BF),
        0,
        7,
        2 * 448 * 512 * 1024,
        name="recv",
    )(arrived, row_pos, mid, out, gain_post, gain_final, stats)
    p1, p2, p3 = move(grad, dy=1), move(grad, dy=-1), move(grad, dy=2)
    q0 = move(grad, dc=1)
    q1, q2, q3 = move(p1, dc=1), move(p2, dc=1), move(p3, dc=1)
    from_y = jnp.stack([y, y, y + 3, y + 3, y + 1, y + 1, y + 2, y + 2]) % 4
    from_c = (c + jnp.array([0, 1] * 4, jnp.int32)) % 2
    heads = (from_y * 2 + from_c).astype(jnp.int32)
    resid_grad, gate_grad, up_grad = call(
        final_kernel,
        (
            jax.ShapeDtypeStruct((448, 512), BF),
            jax.ShapeDtypeStruct((512, 896), BF),
            jax.ShapeDtypeStruct((512, 896), BF),
        ),
        1,
        13,
        2 * 512 * 896 * 3584,
        [
            pltpu.VMEM((8, 464, 512), BF),
            pltpu.VMEM((8, 448, 896), BF),
            pltpu.VMEM((8, 912, 512), BF),
            pltpu.VMEM((2, 512, 896), F32),
            pltpu.VMEM((8, 512), F32),
            pltpu.VMEM((512, 896), F32),
            pltpu.VMEM((448, 512), BF),
            pltpu.VMEM((448, 512), BF),
            pltpu.SemaphoreType.DMA((27,)),
        ],
        name="final",
        space=pl.ANY,
    )(heads, grad, q0, p1, q1, p2, q2, p3, q3, down, bundle, slope, active, stats)
    return (resid_grad.T, gate_grad, up_grad)


def solution(mesh):
    return jax.shard_map(
        per_device,
        mesh=mesh,
        in_specs=(
            P(None, "dp", "head"),
            P(None, "dp", "head"),
            P(None, "dp", "head"),
            P(None, "dp", "head"),
            P(),
            P("dp", "head"),
            P("dp", "head"),
            P("head"),
            P("head"),
            P("dp", "head"),
            P("dp", "head"),
            P("head", "dp"),
        ),
        out_specs=(P("dp", "head"), P("dp", "head"), P("dp", "head")),
        check_vma=False,
    )
```
